32 devices in a mesh: batch: 8 (over z, y), weight: 4 (over x, core).
Axes of the slice: x: 2, y: 2, z: 4, core: 2. Of those that a mesh axis runs over, the one named last changes fastest.
Arguments:
- tokens: bfloat16 [1024, 8192], P(('batch', 'weight')), may hold values from -6 to 6
- segment_ids: int32 [1024], P('batch'), may hold values from 0 to 31, never falling along the last dimension, each value on 1 to 64 neighbouring positions
- norm_gain: float32 [8192], replicated, may hold values from 0.1 to 1.9
- query_weight: bfloat16 [8192, 8192], P('batch', 'weight'), may hold values from -0.0625 to 0.0625
- key_weight: bfloat16 [8192, 1024], P('batch'), may hold values from -0.0625 to 0.0625
- value_weight: bfloat16 [8192, 1024], P('batch'), may hold values from -0.0625 to 0.0625
Outputs:
- attended: bfloat16 [1024, 8192], P('batch', 'weight')
The draws below stay inside these ranges and needn't reach their ends.
Inputs may be any that keep to these rules, and one draw needn't show every extreme that they name: `segment_ids`: segment ids never fall along the tokens; each id covers 1 to 64 consecutive tokens, one of them exactly 64.
All inputs are finite; a program needn't handle non-finite values.
Results may differ from the reference program's by a relative error of at most 0.0079.
Values may be sent and summed in bfloat16 or wider, within the bound.
A program may use at most 128 MiB of HBM per device.

```python
import math
import jax
import jax.numpy as jnp
import numpy as np
from jax import lax

D = 8192
HEADS = 64
KV_HEADS = 8
HEAD_DIM = 128
MOST = 64
PACK = 128
TOKENS = 1024
SEGMENTS = 32


def shard_levels(stream_key, shape, shards, smallest, top_value):
    loudness = 1.0
    for dim, parts in shards:
        steps = jax.random.uniform(jax.random.fold_in(jax.random.fold_in(stream_key, 6), dim), (parts,), jnp.float32, smallest / len(shards), top_value / len(shards))
        loudness = loudness * jnp.repeat(jnp.exp(steps), shape[dim] // parts).reshape((-1,) + (1,) * (len(shape) - 1 - dim))
    return loudness


def length_profile(amount, total, bound, slope):
    loads = [(1 << 20) // math.isqrt(rank ** slope) + 1 for rank in range(2, amount + 1)]
    spare, given = total - bound - (amount - 1), [1] * (amount - 1)
    while spare > 0:
        movable = [i for i in range(amount - 1) if given[i] < bound]
        pool, remaining = sum([loads[i] for i in movable]), spare
        for i in movable:
            addition = min(bound - given[i], max(1, remaining * loads[i] // pool), spare)
            given[i] = given[i] + addition
            spare = spare - addition
    return np.array([bound] + given)


def ragged(rng, count, total, reach, lean):
    if count == 2:
        one = jax.random.randint(rng, (), max(1, total - reach), min(reach, total - 1) + 1)
        return jnp.stack([one, total - one])
    lengths = jnp.asarray(length_profile(count, total, reach, lean), jnp.int32)
    couples = (count - 1) // 2
    giver, taker = lengths[1:1 + 2 * couples:2], lengths[2:2 + 2 * couples:2]
    slack = jnp.minimum(giver - 1, reach - taker)
    moved = jax.random.randint(jax.random.fold_in(rng, 1), (couples,), 0, 1 << 20) % (slack + 1)
    lengths = lengths.at[1:1 + 2 * couples:2].set(giver - moved).at[2:2 + 2 * couples:2].set(taker + moved)
    return lengths[jax.random.permutation(jax.random.fold_in(rng, 2), count)]


def gaussian(key, extent, width, limit, pieces=(), held_as=jnp.bfloat16):
    level = shard_levels(key, extent, pieces, -0.22, 0.18) if pieces else 1.0
    array = jax.random.normal(key, extent, jnp.float32) * width * level
    return jnp.minimum(jnp.maximum(array, -limit), limit).astype(held_as)


def setup_inputs(seed: int = 0) -> dict:
    keys = jax.random.split(jax.random.key(seed), 7)
    tokens = gaussian(keys[0], (TOKENS, D), 1.0, 6.0, ((0, 32),))
    segment_ids = jnp.searchsorted(jnp.cumsum(ragged(keys[1], SEGMENTS, TOKENS, MOST, 2)), jnp.arange(TOKENS), side="right").astype(jnp.int32)
    norm_gain = jnp.clip(1.0 + 0.18 * jax.random.normal(keys[2], (D,), jnp.float32), 0.1, 1.9)
    query_weight = gaussian(keys[3], (D, HEADS * HEAD_DIM), D ** -0.5, 0.0625, ((0, 8), (1, 4)))
    key_weight = gaussian(keys[4], (D, KV_HEADS * HEAD_DIM), D ** -0.5, 0.0625, ((0, 8),))
    value_weight = gaussian(keys[5], (D, KV_HEADS * HEAD_DIM), D ** -0.5, 0.0625, ((0, 8),))
    return dict(tokens=tokens, segment_ids=segment_ids, norm_gain=norm_gain, query_weight=query_weight, key_weight=key_weight, value_weight=value_weight)


ROPE_BASE = 500000.0
EPSILON = 1e-05

def positions_in_segment(seg_ids):
    places = jnp.arange(seg_ids.shape[0], dtype=jnp.int32)
    earlier = jnp.concatenate([seg_ids[:1] - 1, seg_ids[:-1]])
    starts = jnp.where(seg_ids != earlier, places, 0).astype(jnp.int32)
    leading = lax.cummax(starts, axis=0)
    return (places - leading).astype(jnp.int32)

def rotate(vectors, positions):
    half_dim = vectors.shape[-1] // 2
    ratios = jnp.arange(half_dim, dtype=jnp.float32) * (2.0 / vectors.shape[-1])
    frequency = jnp.exp(-math.log(ROPE_BASE) * ratios)
    angles = positions.astype(jnp.float32)[:, None] * frequency[None, :]
    cosine = jnp.cos(angles)[:, None, :]
    sine_part = jnp.sin(angles)[:, None, :]
    front_half = vectors[..., :half_dim]
    back_half = vectors[..., half_dim:]
    return jnp.concatenate([front_half * cosine - back_half * sine_part, back_half * cosine + front_half * sine_part], axis=-1)

def reference(tokens, segment_ids, norm_gain, query_weight, key_weight, value_weight):
    values = tokens.astype(jnp.float32)
    inverse_rms = lax.rsqrt(lax.optimization_barrier(jnp.mean(values * values, axis=1, keepdims=True)) + EPSILON)
    normed = (values * inverse_rms * norm_gain[None, :]).astype(jnp.bfloat16)
    queries = jnp.dot(normed, query_weight, preferred_element_type=jnp.float32)
    key_rows = jnp.dot(normed, key_weight, preferred_element_type=jnp.float32).astype(jnp.bfloat16)
    value_rows = jnp.dot(normed, value_weight, preferred_element_type=jnp.float32).astype(jnp.bfloat16)
    pack_count = TOKENS // PACK
    group_size = HEADS // KV_HEADS

    def one_pack(pack_items):
        query_pack, key_pack, value_pack, seg_ids = pack_items
        positions = positions_in_segment(seg_ids)
        rotated = rotate(query_pack.reshape(PACK, HEADS, HEAD_DIM), positions).astype(jnp.bfloat16)
        rotated_keys = rotate(key_pack.astype(jnp.float32).reshape(PACK, KV_HEADS, HEAD_DIM), positions).astype(jnp.bfloat16)
        grouped = rotated.reshape(PACK, KV_HEADS, group_size, HEAD_DIM).astype(jnp.float32)
        scores = jnp.einsum('ingd,jnd->ngij', grouped, rotated_keys.astype(jnp.float32)) * HEAD_DIM ** (-0.5)
        places = jnp.arange(PACK, dtype=jnp.int32)
        allowed = (seg_ids[:, None] == seg_ids[None, :]) & (places[None, :] <= places[:, None])
        weights = jnp.where(allowed, jnp.exp(scores), 0.0)
        probabilities = (weights / lax.optimization_barrier(jnp.sum(weights, axis=-1, keepdims=True))).astype(jnp.bfloat16)
        mixed = jnp.einsum('ngij,jnd->ingd', probabilities.astype(jnp.float32), value_pack.reshape(PACK, KV_HEADS, HEAD_DIM).astype(jnp.float32))
        return mixed.reshape(PACK, HEADS * HEAD_DIM).astype(jnp.bfloat16)
    stacked = lax.map(one_pack, (queries.reshape(pack_count, PACK, HEADS * HEAD_DIM), key_rows.reshape(pack_count, PACK, KV_HEADS * HEAD_DIM), value_rows.reshape(pack_count, PACK, KV_HEADS * HEAD_DIM), segment_ids.reshape(pack_count, PACK)))
    return stacked.reshape(TOKENS, HEADS * HEAD_DIM)
```

```python
import math

import jax
import jax.numpy as jnp
from jax import lax
from jax.sharding import PartitionSpec as P

HEADS = 64
KV_HEADS = 8
HEAD_DIM = 128


ROPE_BASE = 500000.0
EPSILON = 1e-05


def positions_in_segment(seg_ids):
    places = jnp.arange(seg_ids.shape[0], dtype=jnp.int32)
    earlier = jnp.concatenate([seg_ids[:1] - 1, seg_ids[:-1]])
    starts = jnp.where(seg_ids != earlier, places, 0)
    leading = lax.cummax(starts, axis=0)
    return places - leading


def rotate(vectors, positions):
    half_dim = vectors.shape[-1] // 2
    ratios = jnp.arange(half_dim, dtype=jnp.float32) * (2.0 / vectors.shape[-1])
    frequency = jnp.exp(-math.log(ROPE_BASE) * ratios)
    angles = positions.astype(jnp.float32)[:, None] * frequency[None, :]
    cosine = jnp.cos(angles)[:, None, :]
    sine_part = jnp.sin(angles)[:, None, :]
    front_half = vectors[..., :half_dim]
    back_half = vectors[..., half_dim:]
    return jnp.concatenate(
        [front_half * cosine - back_half * sine_part, back_half * cosine + front_half * sine_part],
        axis=-1,
    )


def attend(grouped, rotated_keys, value_rows, seg_ids):
    scores = jnp.einsum(
        "ingd,jnd->ngij", grouped, rotated_keys, preferred_element_type=jnp.float32
    ) * grouped.shape[-1] ** (-0.5)
    places = jnp.arange(seg_ids.shape[0], dtype=jnp.int32)
    allowed = (seg_ids[:, None] == seg_ids[None, :]) & (places[None, :] <= places[:, None])
    weights = jnp.where(allowed, jnp.exp(scores), 0.0)
    probabilities = (weights / jnp.sum(weights, axis=-1, keepdims=True)).astype(jnp.bfloat16)
    mixed = jnp.einsum(
        "ngij,jnd->ingd", probabilities, value_rows, preferred_element_type=jnp.float32
    )
    return mixed.astype(jnp.bfloat16)


def per_device(tokens, segment_ids, norm_gain, query_weight, key_weight, value_weight):
    head_dim = HEAD_DIM
    query_cols = query_weight.shape[1]
    heads_dev = query_cols // head_dim
    group_size = HEADS // KV_HEADS
    local_kv = max(1, heads_dev // group_size)
    first_kv = lax.axis_index("weight") * heads_dev // group_size
    key_width = local_kv * head_dim
    key_block = lax.dynamic_slice_in_dim(key_weight, first_kv * head_dim, key_width, 1)
    value_block = lax.dynamic_slice_in_dim(value_weight, first_kv * head_dim, key_width, 1)
    values = tokens.astype(jnp.float32)
    inverse_rms = lax.rsqrt(jnp.mean(values * values, axis=1, keepdims=True) + EPSILON)
    normed = (values * inverse_rms * norm_gain[None, :]).astype(jnp.bfloat16)
    batch_size = lax.axis_size("batch")
    weight_size = lax.axis_size("weight")
    own_rows = normed.shape[0]
    slab = query_weight.shape[0]
    mine = lax.all_to_all(normed, "batch", split_axis=1, concat_axis=0, tiled=True)
    spread = lax.all_gather(mine, "weight", axis=0)
    spread = spread.reshape(weight_size, batch_size, own_rows, slab).transpose(1, 0, 2, 3)
    rows = spread.reshape(batch_size * weight_size * own_rows, slab)
    local_weights = jnp.concatenate([query_weight, key_block, value_block], axis=1)
    partial = jnp.dot(rows, local_weights, preferred_element_type=jnp.float32).astype(jnp.bfloat16)
    projected = lax.psum_scatter(partial, "batch", scatter_dimension=0, tiled=True)
    projected = projected.astype(jnp.float32)
    query_part = projected[:, :query_cols]
    key_rows = projected[:, query_cols : query_cols + key_width].astype(jnp.bfloat16)
    value_rows = projected[:, query_cols + key_width :].astype(jnp.bfloat16)
    pack_rows = projected.shape[0]
    positions = positions_in_segment(segment_ids)
    queries = rotate(query_part.reshape(pack_rows, heads_dev, head_dim), positions).astype(
        jnp.bfloat16
    )
    rotated_keys = rotate(
        key_rows.astype(jnp.float32).reshape(pack_rows, local_kv, head_dim), positions
    ).astype(jnp.bfloat16)
    grouped = queries.reshape(pack_rows, local_kv, heads_dev // local_kv, head_dim)
    attended = attend(
        grouped, rotated_keys, value_rows.reshape(pack_rows, local_kv, head_dim), segment_ids
    )
    return attended.reshape(pack_rows, query_cols)


def solution(mesh):
    placed = (
        P(("batch", "weight"), None),
        P("batch"),
        P(),
        P("batch", "weight"),
        P("batch", None),
        P("batch", None),
    )
    return jax.shard_map(
        per_device, mesh=mesh, in_specs=placed, out_specs=P("batch", "weight"), check_vma=False
    )
```

```python
import math

import jax
import jax.numpy as jnp
from jax import lax
from jax.experimental import pallas as pl
from jax.experimental.pallas import tpu as pltpu
from jax.sharding import PartitionSpec as P

HEADS = 64
KV_HEADS = 8
HEAD_DIM = 128


ROPE_BASE = 500000.0
EPSILON = 1e-05


def positions_in_segment(seg_ids):
    places = jnp.arange(seg_ids.shape[0], dtype=jnp.int32)
    earlier = jnp.concatenate([seg_ids[:1] - 1, seg_ids[:-1]])
    starts = jnp.where(seg_ids != earlier, places, 0)
    leading = lax.cummax(starts, axis=0)
    return places - leading


def rotate(vectors, positions):
    half_dim = vectors.shape[-1] // 2
    ratios = jnp.arange(half_dim, dtype=jnp.float32) * (2.0 / vectors.shape[-1])
    frequency = jnp.exp(-math.log(ROPE_BASE) * ratios)
    angles = positions.astype(jnp.float32)[:, None] * frequency[None, :]
    cosine = jnp.cos(angles)[:, None, :]
    sine_part = jnp.sin(angles)[:, None, :]
    front_half = vectors[..., :half_dim]
    back_half = vectors[..., half_dim:]
    return jnp.concatenate(
        [front_half * cosine - back_half * sine_part, back_half * cosine + front_half * sine_part],
        axis=-1,
    )


def attend(grouped, rotated_keys, value_rows, seg_ids):
    scores = jnp.einsum(
        "ingd,jnd->ngij", grouped, rotated_keys, preferred_element_type=jnp.float32
    ) * grouped.shape[-1] ** (-0.5)
    places = jnp.arange(seg_ids.shape[0], dtype=jnp.int32)
    allowed = (seg_ids[:, None] == seg_ids[None, :]) & (places[None, :] <= places[:, None])
    weights = jnp.where(allowed, jnp.exp(scores), 0.0)
    probabilities = (weights / jnp.sum(weights, axis=-1, keepdims=True)).astype(jnp.bfloat16)
    mixed = jnp.einsum(
        "ngij,jnd->ingd", probabilities, value_rows, preferred_element_type=jnp.float32
    )
    return mixed.astype(jnp.bfloat16)


MESH = pl.DeviceIdType.MESH
TILE = 512


def project_kernel(
    tokens_ref, gain_ref, query_ref, key_ref, value_ref, out_ref,
    weights, normed, rows, own, y_out, y_in, z_out, z_in,
    load_sem, tok_send, tok_recv, x_send, core_send, relay_send,
    y_send, y_recv, z_send, z_recv,
):
    me_b = lax.axis_index("batch")
    me_w = lax.axis_index("weight")
    z, y = me_b // 2, me_b % 2
    count, features = tokens_ref.shape
    slab = query_ref.shape[0]
    pack = 4 * count
    tiles = weights.shape[0]
    q_tiles = tiles - 1
    kv = TILE // 2

    order = [(z + 2) % 4, 3 - z, z + 1 - 2 * (z % 2), z]
    other_y = 1 - y
    sources = [(zz * 2 + y, zz * 2 + other_y) for zz in order]
    peers = [b for pair in sources for b in pair]
    x_w, core_w, far_w = (me_w + 2) % 4, me_w + 1 - 2 * (me_w % 2), 3 - me_w

    barrier = pltpu.get_barrier_semaphore()
    for i, b in enumerate(peers):
        if i != 6:
            pl.semaphore_signal(barrier, inc=1, device_id=(b, me_w), device_id_type=MESH)
    for w in (x_w, core_w):
        pl.semaphore_signal(barrier, inc=1, device_id=(me_b, w), device_id_type=MESH)

    loads = [
        pltpu.make_async_copy(
            query_ref.at[:, pl.ds(t * TILE, TILE)], weights.at[t], load_sem.at[t]
        )
        for t in range(q_tiles)
    ]
    first = pl.ds(pl.multiple_of(me_w * kv, kv), kv)
    loads.append(
        pltpu.make_async_copy(
            key_ref.at[:, first], weights.at[q_tiles, :, pl.ds(0, kv)], load_sem.at[q_tiles]
        )
    )
    loads.append(
        pltpu.make_async_copy(
            value_ref.at[:, first], weights.at[q_tiles, :, pl.ds(kv, kv)], load_sem.at[tiles]
        )
    )
    for load in loads:
        load.start()

    total = jnp.zeros((count, 1), jnp.float32)
    for k in range(features // slab):
        part = tokens_ref[:, k * slab : (k + 1) * slab].astype(jnp.float32)
        total = total + jnp.sum(part * part, axis=1, keepdims=True)
    inverse_rms = lax.rsqrt(total * (1.0 / features) + EPSILON)
    for k in range(features // slab):
        part = tokens_ref[:, k * slab : (k + 1) * slab].astype(jnp.float32)
        normed[k] = (part * inverse_rms * gain_ref[:, k * slab : (k + 1) * slab]).astype(jnp.bfloat16)

    def slot(b, w):
        return b * 4 + w

    def at_slot(s):
        return rows.at[pl.ds(pl.multiple_of(s * count, count), count)]

    def send(src, s, device, send_sem):
        return pltpu.make_async_remote_copy(
            src_ref=src, dst_ref=at_slot(s), send_sem=send_sem, recv_sem=tok_recv.at[s],
            device_id=device, device_id_type=MESH,
        )

    def arrived(s):
        send(at_slot(s), s, (me_b, x_w), x_send.at[0]).wait_recv()

    pl.semaphore_wait(barrier, 9)
    mine = slot(me_b, me_w)
    sent = []
    for i, b in enumerate(peers):
        if i != 6:
            copy = send(normed.at[b], mine, (b, me_w), tok_send.at[i])
            copy.start()
            sent.append(copy)
    rows[pl.ds(pl.multiple_of(mine * count, count), count), :] = normed[me_b]

    def forward(i):
        b = peers[i]
        s = slot(b, me_w)
        if i != 6:
            arrived(s)
        for w, sem in ((x_w, x_send), (core_w, core_send)):
            copy = send(at_slot(s), s, (me_b, w), sem.at[i])
            copy.start()
            sent.append(copy)

    def relay(i):
        s = slot(peers[i], x_w)
        arrived(s)
        copy = send(at_slot(s), s, (me_b, core_w), relay_send.at[i])
        copy.start()
        sent.append(copy)

    def collect(i):
        arrived(slot(peers[i], core_w))
        arrived(slot(peers[i], far_w))

    own_rows = pl.ds(pl.multiple_of(y * pack, pack), pack)
    other_rows = pl.ds(pl.multiple_of(other_y * pack, pack), pack)

    def y_copy(c, t):
        return pltpu.make_async_remote_copy(
            src_ref=y_out.at[c, t], dst_ref=y_in.at[c, t],
            send_sem=y_send.at[c, t], recv_sem=y_recv.at[c, t],
            device_id=(z * 2 + other_y, me_w), device_id_type=MESH,
        )

    def z_copy(c, t):
        return pltpu.make_async_remote_copy(
            src_ref=z_out.at[c, t], dst_ref=z_in.at[c, t],
            send_sem=z_send.at[c, t], recv_sem=z_recv.at[c, t],
            device_id=(order[c] * 2 + y, me_w), device_id_type=MESH,
        )

    def multiply(c):
        chunk = pl.ds(pl.multiple_of(order[c] * 2 * pack, 2 * pack), 2 * pack)

        @pl.loop(0, tiles)
        def _(t):
            own[c, t] = jnp.dot(rows[chunk, :], weights[t], preferred_element_type=jnp.float32)
            y_out[c, t] = own[c, t, other_rows, :].astype(jnp.bfloat16)
            y_copy(c, t).start()

    def pair_sum(c, t):
        y_copy(c, t).wait_recv()
        return own[c, t, own_rows, :] + y_in[c, t].astype(jnp.float32)

    def pass_on(c):
        @pl.loop(0, tiles)
        def _(t):
            z_out[c, t] = pair_sum(c, t).astype(jnp.bfloat16)
            z_copy(c, t).start()

    def bring(c):
        for step in (forward, relay):
            step(2 * c)
            step(2 * c + 1)

    forward(6)
    bring(0)
    for load in loads:
        load.wait()
    for c in (0, 1):
        if c == 1:
            bring(1)
        collect(2 * c)
        collect(2 * c + 1)
        multiply(c)
    bring(2)
    forward(7)
    relay(6)
    relay(7)
    pass_on(0)
    collect(4)
    collect(5)
    multiply(2)
    collect(6)
    collect(7)
    multiply(3)
    pass_on(1)
    pass_on(2)

    @pl.loop(0, tiles)
    def _(t):
        result = pair_sum(3, t)
        for c in range(3):
            z_copy(c, t).wait_recv()
            result = result + z_in[c, t].astype(jnp.float32)
        out_ref[t] = result

    for copy in sent:
        copy.wait_send()

    @pl.loop(0, tiles)
    def _(t):
        for c in range(4):
            y_copy(c, t).wait_send()
        for c in range(3):
            z_copy(c, t).wait_send()


def project_on_slice(tokens, norm_gain, query_weight, key_weight, value_weight):
    count, features = tokens.shape
    slab, query_cols = query_weight.shape
    tiles = query_cols // TILE + 1
    pack = 4 * count
    bf16, f32 = jnp.bfloat16, jnp.float32
    dma = pltpu.SemaphoreType.DMA
    vmem = pl.BlockSpec(memory_space=pltpu.VMEM)
    anywhere = pl.BlockSpec(memory_space=pl.ANY)
    return pl.pallas_call(
        project_kernel,
        out_shape=jax.ShapeDtypeStruct((tiles, pack, TILE), f32),
        in_specs=[vmem, vmem, anywhere, anywhere, anywhere],
        out_specs=vmem,
        scratch_shapes=[
            pltpu.VMEM((tiles, slab, TILE), bf16),
            pltpu.VMEM((8, count, slab), bf16),
            pltpu.VMEM((8 * pack, slab), bf16),
            pltpu.VMEM((4, tiles, 2 * pack, TILE), f32),
            pltpu.VMEM((4, tiles, pack, TILE), bf16),
            pltpu.VMEM((4, tiles, pack, TILE), bf16),
            pltpu.VMEM((3, tiles, pack, TILE), bf16),
            pltpu.VMEM((3, tiles, pack, TILE), bf16),
            dma((tiles + 1,)),
            dma((8,)),
            dma((32,)),
            dma((8,)),
            dma((8,)),
            dma((8,)),
            dma((4, tiles)),
            dma((4, tiles)),
            dma((3, tiles)),
            dma((3, tiles)),
        ],
        compiler_params=pltpu.CompilerParams(
            collective_id=0, has_side_effects=True, vmem_limit_bytes=48 * 1024 * 1024
        ),
        cost_estimate=pl.CostEstimate(
            flops=2 * 8 * pack * slab * tiles * TILE, bytes_accessed=2 * slab * tiles * TILE, transcendentals=0
        ),
    )(tokens, norm_gain[None, :], query_weight, key_weight, value_weight)


def per_device(tokens, segment_ids, norm_gain, query_weight, key_weight, value_weight):
    head_dim = HEAD_DIM
    query_cols = query_weight.shape[1]
    heads_dev = query_cols // head_dim
    group_size = HEADS // KV_HEADS
    local_kv = max(1, heads_dev // group_size)
    first_kv = lax.axis_index("weight") * heads_dev // group_size
    key_width = local_kv * head_dim
    if (lax.axis_size("batch"), lax.axis_size("weight"), 2 * key_width) == (8, 4, TILE):
        tiles = project_on_slice(tokens, norm_gain, query_weight, key_weight, value_weight)
        query_part = tiles[:-1].transpose(1, 0, 2).reshape(tiles.shape[1], query_cols)
        key_rows = tiles[-1, :, :key_width].astype(jnp.bfloat16)
        value_rows = tiles[-1, :, key_width:].astype(jnp.bfloat16)
    else:
        key_block = lax.dynamic_slice_in_dim(key_weight, first_kv * head_dim, key_width, 1)
        value_block = lax.dynamic_slice_in_dim(value_weight, first_kv * head_dim, key_width, 1)
        values = tokens.astype(jnp.float32)
        inverse_rms = lax.rsqrt(jnp.mean(values * values, axis=1, keepdims=True) + EPSILON)
        normed = (values * inverse_rms * norm_gain[None, :]).astype(jnp.bfloat16)
        local_weights = jnp.concatenate([query_weight, key_block, value_block], axis=1)
        full_weights = lax.all_gather(local_weights, "batch", axis=0, tiled=True)
        projected = jnp.dot(
            lax.all_gather(normed, "weight", axis=0, tiled=True),
            full_weights,
            preferred_element_type=jnp.float32,
        )
        query_part = projected[:, :query_cols]
        key_rows = projected[:, query_cols : query_cols + key_width].astype(jnp.bfloat16)
        value_rows = projected[:, query_cols + key_width :].astype(jnp.bfloat16)
    pack_rows = segment_ids.shape[0]
    positions = positions_in_segment(segment_ids)
    queries = rotate(query_part.reshape(pack_rows, heads_dev, head_dim), positions).astype(
        jnp.bfloat16
    )
    rotated_keys = rotate(
        key_rows.astype(jnp.float32).reshape(pack_rows, local_kv, head_dim), positions
    ).astype(jnp.bfloat16)
    grouped = queries.reshape(pack_rows, local_kv, heads_dev // local_kv, head_dim)
    attended = attend(
        grouped, rotated_keys, value_rows.reshape(pack_rows, local_kv, head_dim), segment_ids
    )
    return attended.reshape(pack_rows, query_cols)


def solution(mesh):
    placed = (
        P(("batch", "weight"), None),
        P("batch"),
        P(),
        P("batch", "weight"),
        P("batch", None),
        P("batch", None),
    )
    return jax.shard_map(
        per_device, mesh=mesh, in_specs=placed, out_specs=P("batch", "weight"), check_vma=False
    )
```

```python
import math

import jax
import jax.numpy as jnp
from jax import lax
from jax.experimental import pallas as pl
from jax.experimental.pallas import tpu as pltpu
from jax.sharding import PartitionSpec as P

HEADS = 64
KV_HEADS = 8
HEAD_DIM = 128


ROPE_BASE = 500000.0
EPSILON = 1e-05


def positions_in_segment(seg_ids):
    places = jnp.arange(seg_ids.shape[0], dtype=jnp.int32)
    earlier = jnp.concatenate([seg_ids[:1] - 1, seg_ids[:-1]])
    starts = jnp.where(seg_ids != earlier, places, 0)
    leading = lax.cummax(starts, axis=0)
    return places - leading


def rotate(vectors, positions):
    half_dim = vectors.shape[-1] // 2
    ratios = jnp.arange(half_dim, dtype=jnp.float32) * (2.0 / vectors.shape[-1])
    frequency = jnp.exp(-math.log(ROPE_BASE) * ratios)
    angles = positions.astype(jnp.float32)[:, None] * frequency[None, :]
    cosine = jnp.cos(angles)[:, None, :]
    sine_part = jnp.sin(angles)[:, None, :]
    front_half = vectors[..., :half_dim]
    back_half = vectors[..., half_dim:]
    return jnp.concatenate(
        [front_half * cosine - back_half * sine_part, back_half * cosine + front_half * sine_part],
        axis=-1,
    )


def attend(grouped, rotated_keys, value_rows, seg_ids):
    scores = jnp.einsum(
        "ingd,jnd->ngij", grouped, rotated_keys, preferred_element_type=jnp.float32
    ) * grouped.shape[-1] ** (-0.5)
    places = jnp.arange(seg_ids.shape[0], dtype=jnp.int32)
    allowed = (seg_ids[:, None] == seg_ids[None, :]) & (places[None, :] <= places[:, None])
    weights = jnp.where(allowed, jnp.exp(scores), 0.0)
    probabilities = (weights / jnp.sum(weights, axis=-1, keepdims=True)).astype(jnp.bfloat16)
    mixed = jnp.einsum(
        "ngij,jnd->ingd", probabilities, value_rows, preferred_element_type=jnp.float32
    )
    return mixed.astype(jnp.bfloat16)


MESH = pl.DeviceIdType.MESH
TILE = 512


def project_kernel(
    tokens_ref, gain_ref, query_ref, key_ref, value_ref, out_ref,
    tokens, gain, weights, normed, rows, own, y_out, y_in, near_out, near_in, kv_out, kv_in, mid_out, mid_in,
    load_sem, tok_send, tok_recv, x_send, core_send, relay_send,
    y_send, y_recv, near_send, near_recv, kv_send, kv_recv, mid_send, mid_recv,
):
    me_b = lax.axis_index("batch")
    me_w = lax.axis_index("weight")
    z, y = me_b // 2, me_b % 2
    count, features = tokens_ref.shape
    slab = query_ref.shape[0]
    pack = 4 * count
    tiles = weights.shape[0]
    q_tiles = tiles - 1
    kv = TILE // 2

    near_z, mid_z = z + 1 - 2 * (z % 2), (z + 2) % 4
    order = [z, 3 - z, mid_z, near_z]
    other_y = 1 - y
    sources = [(zz * 2 + y, zz * 2 + other_y) for zz in order]
    peers = [b for pair in sources for b in pair]
    x_w, core_w, far_w = (me_w + 2) % 4, me_w + 1 - 2 * (me_w % 2), 3 - me_w

    barrier = pltpu.get_barrier_semaphore()
    for i, b in enumerate(peers):
        if i != 0:
            pl.semaphore_signal(barrier, inc=1, device_id=(b, me_w), device_id_type=MESH)
    for w in (x_w, core_w):
        pl.semaphore_signal(barrier, inc=1, device_id=(me_b, w), device_id_type=MESH)

    token_load = pltpu.make_async_copy(tokens_ref, tokens, load_sem.at[tiles + 1])
    gain_load = pltpu.make_async_copy(gain_ref, gain, load_sem.at[tiles + 2])
    token_load.start()
    gain_load.start()
    loads = [
        pltpu.make_async_copy(
            query_ref.at[:, pl.ds(t * TILE, TILE)], weights.at[t], load_sem.at[t]
        )
        for t in range(q_tiles)
    ]
    first = pl.ds(pl.multiple_of(me_w * kv, kv), kv)
    loads.append(
        pltpu.make_async_copy(
            key_ref.at[:, first], weights.at[q_tiles, :, pl.ds(0, kv)], load_sem.at[q_tiles]
        )
    )
    loads.append(
        pltpu.make_async_copy(
            value_ref.at[:, first], weights.at[q_tiles, :, pl.ds(kv, kv)], load_sem.at[tiles]
        )
    )
    for load in loads:
        load.start()

    token_load.wait()
    gain_load.wait()
    total = jnp.zeros((count, 1), jnp.float32)
    for k in range(features // slab):
        part = tokens[:, k * slab : (k + 1) * slab].astype(jnp.float32)
        total = total + jnp.sum(part * part, axis=1, keepdims=True)
    inverse_rms = lax.rsqrt(total * (1.0 / features) + EPSILON)
    for k in range(features // slab):
        part = tokens[:, k * slab : (k + 1) * slab].astype(jnp.float32)
        normed[k] = (part * inverse_rms * gain[:, k * slab : (k + 1) * slab]).astype(jnp.bfloat16)

    def slot(b, w):
        return b * 4 + w

    def at_slot(s):
        return rows.at[pl.ds(pl.multiple_of(s * count, count), count)]

    def send(src, s, device, send_sem):
        return pltpu.make_async_remote_copy(
            src_ref=src, dst_ref=at_slot(s), send_sem=send_sem, recv_sem=tok_recv.at[s],
            device_id=device, device_id_type=MESH,
        )

    def arrived(s):
        send(at_slot(s), s, (me_b, x_w), x_send.at[0]).wait_recv()

    pl.semaphore_wait(barrier, 9)
    mine = slot(me_b, me_w)
    sent = []
    for i, b in enumerate(peers):
        if i != 0:
            copy = send(normed.at[b], mine, (b, me_w), tok_send.at[i])
            copy.start()
            sent.append(copy)
    rows[pl.ds(pl.multiple_of(mine * count, count), count), :] = normed[me_b]

    def forward(i):
        b = peers[i]
        s = slot(b, me_w)
        if i != 0:
            arrived(s)
        for w, sem in ((x_w, x_send), (core_w, core_send)):
            copy = send(at_slot(s), s, (me_b, w), sem.at[i])
            copy.start()
            sent.append(copy)

    def relay(i):
        s = slot(peers[i], x_w)
        arrived(s)
        copy = send(at_slot(s), s, (me_b, core_w), relay_send.at[i])
        copy.start()
        sent.append(copy)

    def collect(i):
        arrived(slot(peers[i], core_w))
        arrived(slot(peers[i], far_w))

    own_rows = pl.ds(pl.multiple_of(y * pack, pack), pack)
    other_rows = pl.ds(pl.multiple_of(other_y * pack, pack), pack)

    def y_copy(c, t):
        return pltpu.make_async_remote_copy(
            src_ref=y_out.at[c, t], dst_ref=y_in.at[c, t],
            send_sem=y_send.at[c, t], recv_sem=y_recv.at[c, t],
            device_id=(z * 2 + other_y, me_w), device_id_type=MESH,
        )

    def near_copy(j, t):
        return pltpu.make_async_remote_copy(
            src_ref=near_out.at[j, t], dst_ref=near_in.at[j, t],
            send_sem=near_send.at[j, t], recv_sem=near_recv.at[j, t],
            device_id=(near_z * 2 + y, me_w), device_id_type=MESH,
        )

    def kv_copy(j):
        return pltpu.make_async_remote_copy(
            src_ref=kv_out.at[j], dst_ref=kv_in.at[j],
            send_sem=kv_send.at[j], recv_sem=kv_recv.at[j],
            device_id=(near_z * 2 + y, me_w), device_id_type=MESH,
        )

    def mid_copy(t):
        return pltpu.make_async_remote_copy(
            src_ref=mid_out.at[t], dst_ref=mid_in.at[t],
            send_sem=mid_send.at[t], recv_sem=mid_recv.at[t],
            device_id=(mid_z * 2 + y, me_w), device_id_type=MESH,
        )

    def chunk(c):
        return pl.ds(pl.multiple_of(order[c] * 2 * pack, 2 * pack), 2 * pack)

    def product(c, t):
        return jnp.dot(rows[chunk(c), :], weights[t], preferred_element_type=jnp.float32)

    def multiply_kv(c):
        if c % 2:
            kv_out[c // 2] = product(c, q_tiles).astype(jnp.bfloat16)
            kv_copy(c // 2).start()
        else:
            own[c, q_tiles] = product(c, q_tiles)

    def multiply(c):
        @pl.loop(0, q_tiles)
        def _(t):
            own[c, t] = product(c, t)
            y_out[c, t] = own[c, t, other_rows, :].astype(jnp.bfloat16)
            y_copy(c, t).start()

    def pair_sum(c, t):
        y_copy(c, t).wait_recv()
        return own[c, t, own_rows, :] + y_in[c, t].astype(jnp.float32)

    def pass_near(j):
        @pl.loop(0, q_tiles)
        def _(t):
            near_out[j, t] = pair_sum(2 * j + 1, t).astype(jnp.bfloat16)
            near_copy(j, t).start()

    def ready(c):
        for step in (forward, relay, collect):
            step(2 * c)
            step(2 * c + 1)

    ready(0)
    for load in loads:
        load.wait()
    multiply(0)
    ready(1)
    multiply_kv(1)
    multiply(1)
    ready(2)
    multiply(2)
    ready(3)
    multiply_kv(3)
    multiply_kv(2)
    multiply_kv(0)
    for c, j in ((2, 0), (0, 1)):
        kv_copy(j).wait_recv()
        own[c, q_tiles] = own[c, q_tiles] + kv_in[j].astype(jnp.float32)
        y_out[c, q_tiles] = own[c, q_tiles, other_rows, :].astype(jnp.bfloat16)
        y_copy(c, q_tiles).start()
    multiply(3)
    pass_near(0)

    @pl.loop(0, q_tiles)
    def _(t):
        total = pair_sum(2, t)
        near_copy(0, t).wait_recv()
        mid_out[t] = (total + near_in[0, t].astype(jnp.float32)).astype(jnp.bfloat16)
        mid_copy(t).start()

    mid_out[q_tiles] = pair_sum(2, q_tiles).astype(jnp.bfloat16)
    mid_copy(q_tiles).start()
    pass_near(1)

    kv_total = pair_sum(0, q_tiles)
    mid_copy(q_tiles).wait_recv()
    out_ref[q_tiles] = kv_total + mid_in[q_tiles].astype(jnp.float32)

    @pl.loop(0, q_tiles)
    def _(t):
        total = pair_sum(0, t)
        mid_copy(t).wait_recv()
        total = total + mid_in[t].astype(jnp.float32)
        near_copy(1, t).wait_recv()
        out_ref[t] = total + near_in[1, t].astype(jnp.float32)

    for copy in sent:
        copy.wait_send()

    @pl.loop(0, q_tiles)
    def _(t):
        for c in range(4):
            y_copy(c, t).wait_send()
        for j in range(2):
            near_copy(j, t).wait_send()
        mid_copy(t).wait_send()

    for j in range(2):
        kv_copy(j).wait_send()
        y_copy(2 * j, q_tiles).wait_send()
    mid_copy(q_tiles).wait_send()


def project_on_slice(tokens, norm_gain, query_weight, key_weight, value_weight):
    count, features = tokens.shape
    slab, query_cols = query_weight.shape
    tiles = query_cols // TILE + 1
    pack = 4 * count
    bf16, f32 = jnp.bfloat16, jnp.float32
    dma = pltpu.SemaphoreType.DMA
    vmem = pl.BlockSpec(memory_space=pltpu.VMEM)
    hbm = pl.BlockSpec(memory_space=pltpu.HBM)
    return pl.pallas_call(
        project_kernel,
        out_shape=jax.ShapeDtypeStruct((tiles, pack, TILE), f32),
        in_specs=[hbm] * 5,
        out_specs=vmem,
        scratch_shapes=[
            pltpu.VMEM((count, features), bf16),
            pltpu.VMEM((1, features), f32),
            pltpu.VMEM((tiles, slab, TILE), bf16),
            pltpu.VMEM((8, count, slab), bf16),
            pltpu.VMEM((8 * pack, slab), bf16),
            pltpu.VMEM((4, tiles, 2 * pack, TILE), f32),
            pltpu.VMEM((4, tiles, pack, TILE), bf16),
            pltpu.VMEM((4, tiles, pack, TILE), bf16),
            pltpu.VMEM((2, tiles - 1, pack, TILE), bf16),
            pltpu.VMEM((2, tiles - 1, pack, TILE), bf16),
            pltpu.VMEM((2, 2 * pack, TILE), bf16),
            pltpu.VMEM((2, 2 * pack, TILE), bf16),
            pltpu.VMEM((tiles, pack, TILE), bf16),
            pltpu.VMEM((tiles, pack, TILE), bf16),
            dma((tiles + 3,)),
            dma((8,)),
            dma((32,)),
            dma((8,)),
            dma((8,)),
            dma((8,)),
            dma((4, tiles)),
            dma((4, tiles)),
            dma((2, tiles - 1)),
            dma((2, tiles - 1)),
            dma((2,)),
            dma((2,)),
            dma((tiles,)),
            dma((tiles,)),
        ],
        compiler_params=pltpu.CompilerParams(
            collective_id=0, has_side_effects=True, vmem_limit_bytes=56 * 1024 * 1024
        ),
        cost_estimate=pl.CostEstimate(
            flops=2 * 8 * pack * slab * tiles * TILE, bytes_accessed=2 * slab * tiles * TILE, transcendentals=0
        ),
    )(tokens, norm_gain[None, :], query_weight, key_weight, value_weight)


def per_device(tokens, segment_ids, norm_gain, query_weight, key_weight, value_weight):
    head_dim = HEAD_DIM
    query_cols = query_weight.shape[1]
    heads_dev = query_cols // head_dim
    group_size = HEADS // KV_HEADS
    local_kv = max(1, heads_dev // group_size)
    first_kv = lax.axis_index("weight") * heads_dev // group_size
    key_width = local_kv * head_dim
    if (lax.axis_size("batch"), lax.axis_size("weight"), 2 * key_width) == (8, 4, TILE):
        tiles = project_on_slice(tokens, norm_gain, query_weight, key_weight, value_weight)
        query_part = tiles[:-1].transpose(1, 0, 2).reshape(tiles.shape[1], query_cols)
        key_rows = tiles[-1, :, :key_width].astype(jnp.bfloat16)
        value_rows = tiles[-1, :, key_width:].astype(jnp.bfloat16)
    else:
        key_block = lax.dynamic_slice_in_dim(key_weight, first_kv * head_dim, key_width, 1)
        value_block = lax.dynamic_slice_in_dim(value_weight, first_kv * head_dim, key_width, 1)
        values = tokens.astype(jnp.float32)
        inverse_rms = lax.rsqrt(jnp.mean(values * values, axis=1, keepdims=True) + EPSILON)
        normed = (values * inverse_rms * norm_gain[None, :]).astype(jnp.bfloat16)
        local_weights = jnp.concatenate([query_weight, key_block, value_block], axis=1)
        full_weights = lax.all_gather(local_weights, "batch", axis=0, tiled=True)
        projected = jnp.dot(
            lax.all_gather(normed, "weight", axis=0, tiled=True),
            full_weights,
            preferred_element_type=jnp.float32,
        )
        query_part = projected[:, :query_cols]
        key_rows = projected[:, query_cols : query_cols + key_width].astype(jnp.bfloat16)
        value_rows = projected[:, query_cols + key_width :].astype(jnp.bfloat16)
    pack_rows = segment_ids.shape[0]
    positions = positions_in_segment(segment_ids)
    queries = rotate(query_part.reshape(pack_rows, heads_dev, head_dim), positions).astype(
        jnp.bfloat16
    )
    rotated_keys = rotate(
        key_rows.astype(jnp.float32).reshape(pack_rows, local_kv, head_dim), positions
    ).astype(jnp.bfloat16)
    grouped = queries.reshape(pack_rows, local_kv, heads_dev // local_kv, head_dim)
    attended = attend(
        grouped, rotated_keys, value_rows.reshape(pack_rows, local_kv, head_dim), segment_ids
    )
    return attended.reshape(pack_rows, query_cols)


def solution(mesh):
    placed = (
        P(("batch", "weight"), None),
        P("batch"),
        P(),
        P("batch", "weight"),
        P("batch", None),
        P("batch", None),
    )
    return jax.shard_map(
        per_device, mesh=mesh, in_specs=placed, out_specs=P("batch", "weight"), check_vma=False
    )
```

```python
import math

import jax
import jax.numpy as jnp
from jax import lax
from jax.experimental import pallas as pl
from jax.experimental.pallas import tpu as pltpu
from jax.sharding import PartitionSpec as P

HEADS = 64
KV_HEADS = 8
HEAD_DIM = 128


ROPE_BASE = 500000.0
EPSILON = 1e-05


def positions_in_segment(seg_ids):
    places = jnp.arange(seg_ids.shape[0], dtype=jnp.int32)
    earlier = jnp.concatenate([seg_ids[:1] - 1, seg_ids[:-1]])
    starts = jnp.where(seg_ids != earlier, places, 0)
    leading = lax.cummax(starts, axis=0)
    return places - leading


def rotate(vectors, positions):
    half_dim = vectors.shape[-1] // 2
    ratios = jnp.arange(half_dim, dtype=jnp.float32) * (2.0 / vectors.shape[-1])
    frequency = jnp.exp(-math.log(ROPE_BASE) * ratios)
    angles = positions.astype(jnp.float32)[:, None] * frequency[None, :]
    cosine = jnp.cos(angles)[:, None, :]
    sine_part = jnp.sin(angles)[:, None, :]
    front_half = vectors[..., :half_dim]
    back_half = vectors[..., half_dim:]
    return jnp.concatenate(
        [front_half * cosine - back_half * sine_part, back_half * cosine + front_half * sine_part],
        axis=-1,
    )


def attend(grouped, rotated_keys, value_rows, seg_ids):
    scores = jnp.einsum(
        "ingd,jnd->ngij", grouped, rotated_keys, preferred_element_type=jnp.float32
    ) * grouped.shape[-1] ** (-0.5)
    places = jnp.arange(seg_ids.shape[0], dtype=jnp.int32)
    allowed = (seg_ids[:, None] == seg_ids[None, :]) & (places[None, :] <= places[:, None])
    weights = jnp.where(allowed, jnp.exp(scores), 0.0)
    probabilities = (weights / jnp.sum(weights, axis=-1, keepdims=True)).astype(jnp.bfloat16)
    mixed = jnp.einsum(
        "ngij,jnd->ingd", probabilities, value_rows, preferred_element_type=jnp.float32
    )
    return mixed.astype(jnp.bfloat16)


MESH = pl.DeviceIdType.MESH
TILE = 512


def project_kernel(
    tokens_ref, gain_ref, query_ref, key_ref, value_ref, out_ref,
    tokens, gain, weights, normed, rows, own, y_out, y_in, near_out, near_in, kv_out, kv_in, mid_out, mid_in,
    load_sem, tok_send, tok_recv, x_send, core_send, relay_send,
    y_send, y_recv, near_send, near_recv, kv_send, kv_recv, mid_send, mid_recv,
):
    me_b = lax.axis_index("batch")
    me_w = lax.axis_index("weight")
    z, y = me_b // 2, me_b % 2
    count, features = tokens_ref.shape
    slab = query_ref.shape[0]
    pack = 4 * count
    tiles = weights.shape[0]
    q_tiles = tiles - 1
    kv = TILE // 2

    near_z, mid_z = z + 1 - 2 * (z % 2), (z + 2) % 4
    order = [z, 3 - z, mid_z, near_z]
    other_y = 1 - y
    sources = [(zz * 2 + y, zz * 2 + other_y) for zz in order]
    peers = [b for pair in sources for b in pair]
    x_w, core_w, far_w = (me_w + 2) % 4, me_w + 1 - 2 * (me_w % 2), 3 - me_w

    barrier = pltpu.get_barrier_semaphore()
    for i, b in enumerate(peers):
        if i != 0:
            pl.semaphore_signal(barrier, inc=1, device_id=(b, me_w), device_id_type=MESH)
    for w in (x_w, core_w):
        pl.semaphore_signal(barrier, inc=1, device_id=(me_b, w), device_id_type=MESH)

    token_load = pltpu.make_async_copy(tokens_ref, tokens, load_sem.at[tiles + 1])
    gain_load = pltpu.make_async_copy(gain_ref, gain, load_sem.at[tiles + 2])
    token_load.start()
    gain_load.start()
    loads = [
        pltpu.make_async_copy(
            query_ref.at[:, pl.ds(t * TILE, TILE)], weights.at[t], load_sem.at[t]
        )
        for t in range(q_tiles)
    ]
    first = pl.ds(pl.multiple_of(me_w * kv, kv), kv)
    loads.append(
        pltpu.make_async_copy(
            key_ref.at[:, first], weights.at[q_tiles, :, pl.ds(0, kv)], load_sem.at[q_tiles]
        )
    )
    loads.append(
        pltpu.make_async_copy(
            value_ref.at[:, first], weights.at[q_tiles, :, pl.ds(kv, kv)], load_sem.at[tiles]
        )
    )
    for load in loads:
        load.start()

    token_load.wait()
    gain_load.wait()
    total = jnp.zeros((count, 1), jnp.float32)
    for k in range(features // slab):
        part = tokens[:, k * slab : (k + 1) * slab].astype(jnp.float32)
        total = total + jnp.sum(part * part, axis=1, keepdims=True)
    inverse_rms = lax.rsqrt(total * (1.0 / features) + EPSILON)
    for k in range(features // slab):
        part = tokens[:, k * slab : (k + 1) * slab].astype(jnp.float32)
        normed[k] = (part * inverse_rms * gain[:, k * slab : (k + 1) * slab]).astype(jnp.bfloat16)

    def slot(b, w):
        return b * 4 + w

    def at_slot(s):
        return rows.at[pl.ds(pl.multiple_of(s * count, count), count)]

    def send(src, s, device, send_sem):
        return pltpu.make_async_remote_copy(
            src_ref=src, dst_ref=at_slot(s), send_sem=send_sem, recv_sem=tok_recv.at[s],
            device_id=device, device_id_type=MESH,
        )

    def arrived(s):
        send(at_slot(s), s, (me_b, x_w), x_send.at[0]).wait_recv()

    pl.semaphore_wait(barrier, 9)
    mine = slot(me_b, me_w)
    sent = []
    for i, b in enumerate(peers):
        if i != 0:
            copy = send(normed.at[b], mine, (b, me_w), tok_send.at[i])
            copy.start()
            sent.append(copy)
    rows[pl.ds(pl.multiple_of(mine * count, count), count), :] = normed[me_b]

    def forward(i):
        b = peers[i]
        s = slot(b, me_w)
        if i != 0:
            arrived(s)
        for w, sem in ((x_w, x_send), (core_w, core_send)):
            copy = send(at_slot(s), s, (me_b, w), sem.at[i])
            copy.start()
            sent.append(copy)

    def relay(i):
        s = slot(peers[i], x_w)
        arrived(s)
        copy = send(at_slot(s), s, (me_b, core_w), relay_send.at[i])
        copy.start()
        sent.append(copy)

    def collect(i):
        arrived(slot(peers[i], core_w))
        arrived(slot(peers[i], far_w))

    own_rows = pl.ds(pl.multiple_of(y * pack, pack), pack)
    other_rows = pl.ds(pl.multiple_of(other_y * pack, pack), pack)

    def y_copy(c, t):
        return pltpu.make_async_remote_copy(
            src_ref=y_out.at[c, t], dst_ref=y_in.at[c, t],
            send_sem=y_send.at[c, t], recv_sem=y_recv.at[c, t],
            device_id=(z * 2 + other_y, me_w), device_id_type=MESH,
        )

    def near_copy(j, t):
        return pltpu.make_async_remote_copy(
            src_ref=near_out.at[j, t], dst_ref=near_in.at[j, t],
            send_sem=near_send.at[j, t], recv_sem=near_recv.at[j, t],
            device_id=(near_z * 2 + y, me_w), device_id_type=MESH,
        )

    def kv_copy(j):
        return pltpu.make_async_remote_copy(
            src_ref=kv_out.at[j], dst_ref=kv_in.at[j],
            send_sem=kv_send.at[j], recv_sem=kv_recv.at[j],
            device_id=(near_z * 2 + y, me_w), device_id_type=MESH,
        )

    def mid_copy(t):
        return pltpu.make_async_remote_copy(
            src_ref=mid_out.at[t], dst_ref=mid_in.at[t],
            send_sem=mid_send.at[t], recv_sem=mid_recv.at[t],
            device_id=(mid_z * 2 + y, me_w), device_id_type=MESH,
        )

    def chunk(c):
        return pl.ds(pl.multiple_of(order[c] * 2 * pack, 2 * pack), 2 * pack)

    def product(c, t):
        return jnp.dot(rows[chunk(c), :], weights[t], preferred_element_type=jnp.float32)

    def multiply_kv(c):
        if c % 2:
            kv_out[c // 2] = product(c, q_tiles).astype(jnp.bfloat16)
            kv_copy(c // 2).start()
        else:
            own[c, q_tiles] = product(c, q_tiles)

    def multiply(c, start):
        @pl.loop(0, q_tiles)
        def _(t):
            own[c, t] = product(c, t)
            y_out[c, t] = own[c, t, other_rows, :].astype(jnp.bfloat16)
            if start:
                y_copy(c, t).start()

    def pair_sum(c, t):
        y_copy(c, t).wait_recv()
        return own[c, t, own_rows, :] + y_in[c, t].astype(jnp.float32)

    def pass_near(j, start_next):
        @pl.loop(0, q_tiles)
        def _(t):
            total = pair_sum(2 * j + 1, t)
            if start_next:
                y_copy(2, t).start()
            near_out[j, t] = total.astype(jnp.bfloat16)
            near_copy(j, t).start()

    def ready(*chunks):
        for step in (forward, relay, collect):
            for c in chunks:
                step(2 * c)
                step(2 * c + 1)

    ready(0)
    for load in loads:
        load.wait()
    multiply(0, True)
    ready(1)
    multiply_kv(1)
    multiply(1, True)
    ready(2, 3)
    multiply_kv(3)
    multiply(2, False)
    multiply_kv(2)
    multiply_kv(0)
    pass_near(0, True)
    multiply(3, False)
    for c, j in ((2, 0), (0, 1)):
        kv_copy(j).wait_recv()
        own[c, q_tiles] = own[c, q_tiles] + kv_in[j].astype(jnp.float32)
        y_out[c, q_tiles] = own[c, q_tiles, other_rows, :].astype(jnp.bfloat16)

    y_later = [(2, q_tiles), (0, q_tiles)] + [(3, t) for t in range(q_tiles)]
    for t in range(q_tiles):
        total = pair_sum(2, t)
        y_copy(*y_later[t]).start()
        near_copy(0, t).wait_recv()
        mid_out[t] = (total + near_in[0, t].astype(jnp.float32)).astype(jnp.bfloat16)
        mid_copy(t).start()

    mid_out[q_tiles] = pair_sum(2, q_tiles).astype(jnp.bfloat16)
    mid_copy(q_tiles).start()
    for later in y_later[q_tiles:]:
        y_copy(*later).start()
    pass_near(1, False)

    kv_total = pair_sum(0, q_tiles)
    mid_copy(q_tiles).wait_recv()
    out_ref[q_tiles] = kv_total + mid_in[q_tiles].astype(jnp.float32)

    @pl.loop(0, q_tiles)
    def _(t):
        total = pair_sum(0, t)
        mid_copy(t).wait_recv()
        total = total + mid_in[t].astype(jnp.float32)
        near_copy(1, t).wait_recv()
        out_ref[t] = total + near_in[1, t].astype(jnp.float32)

    for copy in sent:
        copy.wait_send()

    @pl.loop(0, q_tiles)
    def _(t):
        for c in range(4):
            y_copy(c, t).wait_send()
        for j in range(2):
            near_copy(j, t).wait_send()
        mid_copy(t).wait_send()

    for j in range(2):
        kv_copy(j).wait_send()
        y_copy(2 * j, q_tiles).wait_send()
    mid_copy(q_tiles).wait_send()


def project_on_slice(tokens, norm_gain, query_weight, key_weight, value_weight):
    count, features = tokens.shape
    slab, query_cols = query_weight.shape
    tiles = query_cols // TILE + 1
    pack = 4 * count
    bf16, f32 = jnp.bfloat16, jnp.float32
    dma = pltpu.SemaphoreType.DMA
    vmem = pl.BlockSpec(memory_space=pltpu.VMEM)
    hbm = pl.BlockSpec(memory_space=pltpu.HBM)
    return pl.pallas_call(
        project_kernel,
        out_shape=jax.ShapeDtypeStruct((tiles, pack, TILE), f32),
        in_specs=[hbm] * 5,
        out_specs=vmem,
        scratch_shapes=[
            pltpu.VMEM((count, features), bf16),
            pltpu.VMEM((1, features), f32),
            pltpu.VMEM((tiles, slab, TILE), bf16),
            pltpu.VMEM((8, count, slab), bf16),
            pltpu.VMEM((8 * pack, slab), bf16),
            pltpu.VMEM((4, tiles, 2 * pack, TILE), f32),
            pltpu.VMEM((4, tiles, pack, TILE), bf16),
            pltpu.VMEM((4, tiles, pack, TILE), bf16),
            pltpu.VMEM((2, tiles - 1, pack, TILE), bf16),
            pltpu.VMEM((2, tiles - 1, pack, TILE), bf16),
            pltpu.VMEM((2, 2 * pack, TILE), bf16),
            pltpu.VMEM((2, 2 * pack, TILE), bf16),
            pltpu.VMEM((tiles, pack, TILE), bf16),
            pltpu.VMEM((tiles, pack, TILE), bf16),
            dma((tiles + 3,)),
            dma((8,)),
            dma((32,)),
            dma((8,)),
            dma((8,)),
            dma((8,)),
            dma((4, tiles)),
            dma((4, tiles)),
            dma((2, tiles - 1)),
            dma((2, tiles - 1)),
            dma((2,)),
            dma((2,)),
            dma((tiles,)),
            dma((tiles,)),
        ],
        compiler_params=pltpu.CompilerParams(
            collective_id=0, has_side_effects=True, vmem_limit_bytes=56 * 1024 * 1024
        ),
        cost_estimate=pl.CostEstimate(
            flops=2 * 8 * pack * slab * tiles * TILE, bytes_accessed=2 * slab * tiles * TILE, transcendentals=0
        ),
    )(tokens, norm_gain[None, :], query_weight, key_weight, value_weight)


def per_device(tokens, segment_ids, norm_gain, query_weight, key_weight, value_weight):
    head_dim = HEAD_DIM
    query_cols = query_weight.shape[1]
    heads_dev = query_cols // head_dim
    group_size = HEADS // KV_HEADS
    local_kv = max(1, heads_dev // group_size)
    first_kv = lax.axis_index("weight") * heads_dev // group_size
    key_width = local_kv * head_dim
    if (lax.axis_size("batch"), lax.axis_size("weight"), 2 * key_width) == (8, 4, TILE):
        tiles = project_on_slice(tokens, norm_gain, query_weight, key_weight, value_weight)
        query_part = tiles[:-1].transpose(1, 0, 2).reshape(tiles.shape[1], query_cols)
        key_rows = tiles[-1, :, :key_width].astype(jnp.bfloat16)
        value_rows = tiles[-1, :, key_width:].astype(jnp.bfloat16)
    else:
        key_block = lax.dynamic_slice_in_dim(key_weight, first_kv * head_dim, key_width, 1)
        value_block = lax.dynamic_slice_in_dim(value_weight, first_kv * head_dim, key_width, 1)
        values = tokens.astype(jnp.float32)
        inverse_rms = lax.rsqrt(jnp.mean(values * values, axis=1, keepdims=True) + EPSILON)
        normed = (values * inverse_rms * norm_gain[None, :]).astype(jnp.bfloat16)
        local_weights = jnp.concatenate([query_weight, key_block, value_block], axis=1)
        full_weights = lax.all_gather(local_weights, "batch", axis=0, tiled=True)
        projected = jnp.dot(
            lax.all_gather(normed, "weight", axis=0, tiled=True),
            full_weights,
            preferred_element_type=jnp.float32,
        )
        query_part = projected[:, :query_cols]
        key_rows = projected[:, query_cols : query_cols + key_width].astype(jnp.bfloat16)
        value_rows = projected[:, query_cols + key_width :].astype(jnp.bfloat16)
    pack_rows = segment_ids.shape[0]
    positions = positions_in_segment(segment_ids)
    queries = rotate(query_part.reshape(pack_rows, heads_dev, head_dim), positions).astype(
        jnp.bfloat16
    )
    rotated_keys = rotate(
        key_rows.astype(jnp.float32).reshape(pack_rows, local_kv, head_dim), positions
    ).astype(jnp.bfloat16)
    grouped = queries.reshape(pack_rows, local_kv, heads_dev // local_kv, head_dim)
    attended = attend(
        grouped, rotated_keys, value_rows.reshape(pack_rows, local_kv, head_dim), segment_ids
    )
    return attended.reshape(pack_rows, query_cols)


def solution(mesh):
    placed = (
        P(("batch", "weight"), None),
        P("batch"),
        P(),
        P("batch", "weight"),
        P("batch", None),
        P("batch", None),
    )
    return jax.shard_map(
        per_device, mesh=mesh, in_specs=placed, out_specs=P("batch", "weight"), check_vma=False
    )
```

```python
import math

import jax
import jax.numpy as jnp
from jax import lax
from jax.experimental import pallas as pl
from jax.experimental.pallas import tpu as pltpu
from jax.sharding import PartitionSpec as P

HEADS = 64
KV_HEADS = 8
HEAD_DIM = 128


ROPE_BASE = 500000.0
EPSILON = 1e-05


def positions_in_segment(seg_ids):
    places = jnp.arange(seg_ids.shape[0], dtype=jnp.int32)
    earlier = jnp.concatenate([seg_ids[:1] - 1, seg_ids[:-1]])
    starts = jnp.where(seg_ids != earlier, places, 0)
    leading = lax.cummax(starts, axis=0)
    return places - leading


def rope_tables(positions, head_dim):
    ratios = jnp.arange(head_dim // 2, dtype=jnp.float32) * (2.0 / head_dim)
    frequency = jnp.exp(-math.log(ROPE_BASE) * ratios)
    angles = positions.astype(jnp.float32)[:, None] * frequency[None, :]
    return jnp.cos(angles), jnp.sin(angles)


def rotate(vectors, positions):
    half_dim = vectors.shape[-1] // 2
    cosine, sine_part = rope_tables(positions, vectors.shape[-1])
    cosine, sine_part = cosine[:, None, :], sine_part[:, None, :]
    front_half = vectors[..., :half_dim]
    back_half = vectors[..., half_dim:]
    return jnp.concatenate(
        [front_half * cosine - back_half * sine_part, back_half * cosine + front_half * sine_part],
        axis=-1,
    )


def attend(grouped, rotated_keys, value_rows, seg_ids):
    scores = jnp.einsum(
        "ingd,jnd->ngij", grouped, rotated_keys, preferred_element_type=jnp.float32
    ) * grouped.shape[-1] ** (-0.5)
    places = jnp.arange(seg_ids.shape[0], dtype=jnp.int32)
    allowed = (seg_ids[:, None] == seg_ids[None, :]) & (places[None, :] <= places[:, None])
    weights = jnp.where(allowed, jnp.exp(scores), 0.0)
    probabilities = (weights / jnp.sum(weights, axis=-1, keepdims=True)).astype(jnp.bfloat16)
    mixed = jnp.einsum(
        "ngij,jnd->ingd", probabilities, value_rows, preferred_element_type=jnp.float32
    )
    return mixed.astype(jnp.bfloat16)


MESH = pl.DeviceIdType.MESH
TILE = 512


def attend_kernel(
    tokens_ref, gain_ref, query_ref, key_ref, value_ref, cosine_ref, sine_ref, seg_col_ref, seg_row_ref, out_ref,
    tokens, gain, weights, normed, rows, own, y_out, y_in, near_out, near_in, kv_out, kv_in, mid_out, mid_in, held_keys, held_values,
    load_sem, tok_send, tok_recv, x_send, core_send, relay_send,
    y_send, y_recv, near_send, near_recv, kv_send, kv_recv, mid_send, mid_recv,
):
    me_b = lax.axis_index("batch")
    me_w = lax.axis_index("weight")
    z, y = me_b // 2, me_b % 2
    count, features = tokens_ref.shape
    slab = query_ref.shape[0]
    pack = 4 * count
    tiles = weights.shape[0]
    q_tiles = tiles - 1
    kv = TILE // 2

    near_z, mid_z = z + 1 - 2 * (z % 2), (z + 2) % 4
    order = [z, 3 - z, mid_z, near_z]
    other_y = 1 - y
    sources = [(zz * 2 + y, zz * 2 + other_y) for zz in order]
    peers = [b for pair in sources for b in pair]
    x_w, core_w, far_w = (me_w + 2) % 4, me_w + 1 - 2 * (me_w % 2), 3 - me_w

    barrier = pltpu.get_barrier_semaphore()
    for i, b in enumerate(peers):
        if i != 0:
            pl.semaphore_signal(barrier, inc=1, device_id=(b, me_w), device_id_type=MESH)
    for w in (x_w, core_w):
        pl.semaphore_signal(barrier, inc=1, device_id=(me_b, w), device_id_type=MESH)

    token_load = pltpu.make_async_copy(tokens_ref, tokens, load_sem.at[tiles + 1])
    gain_load = pltpu.make_async_copy(gain_ref, gain, load_sem.at[tiles + 2])
    token_load.start()
    gain_load.start()
    loads = [
        pltpu.make_async_copy(
            query_ref.at[:, pl.ds(t * TILE, TILE)], weights.at[t], load_sem.at[t]
        )
        for t in range(q_tiles)
    ]
    first = pl.ds(pl.multiple_of(me_w * kv, kv), kv)
    loads.append(
        pltpu.make_async_copy(
            key_ref.at[:, first], weights.at[q_tiles, :, pl.ds(0, kv)], load_sem.at[q_tiles]
        )
    )
    loads.append(
        pltpu.make_async_copy(
            value_ref.at[:, first], weights.at[q_tiles, :, pl.ds(kv, kv)], load_sem.at[tiles]
        )
    )
    for load in loads:
        load.start()

    token_load.wait()
    gain_load.wait()
    total = jnp.zeros((count, 1), jnp.float32)
    for k in range(features // slab):
        part = tokens[:, k * slab : (k + 1) * slab].astype(jnp.float32)
        total = total + jnp.sum(part * part, axis=1, keepdims=True)
    inverse_rms = lax.rsqrt(total * (1.0 / features) + EPSILON)
    for k in range(features // slab):
        part = tokens[:, k * slab : (k + 1) * slab].astype(jnp.float32)
        normed[k] = (part * inverse_rms * gain[:, k * slab : (k + 1) * slab]).astype(jnp.bfloat16)

    def slot(b, w):
        return b * 4 + w

    def at_slot(s):
        return rows.at[pl.ds(pl.multiple_of(s * count, count), count)]

    def send(src, s, device, send_sem):
        return pltpu.make_async_remote_copy(
            src_ref=src, dst_ref=at_slot(s), send_sem=send_sem, recv_sem=tok_recv.at[s],
            device_id=device, device_id_type=MESH,
        )

    def arrived(s):
        send(at_slot(s), s, (me_b, x_w), x_send.at[0]).wait_recv()

    pl.semaphore_wait(barrier, 9)
    mine = slot(me_b, me_w)
    sent = []
    for i, b in enumerate(peers):
        if i != 0:
            copy = send(normed.at[b], mine, (b, me_w), tok_send.at[i])
            copy.start()
            sent.append(copy)
    rows[pl.ds(pl.multiple_of(mine * count, count), count), :] = normed[me_b]

    def forward(i):
        b = peers[i]
        s = slot(b, me_w)
        if i != 0:
            arrived(s)
        for w, sem in ((x_w, x_send), (core_w, core_send)):
            copy = send(at_slot(s), s, (me_b, w), sem.at[i])
            copy.start()
            sent.append(copy)

    def relay(i):
        s = slot(peers[i], x_w)
        arrived(s)
        copy = send(at_slot(s), s, (me_b, core_w), relay_send.at[i])
        copy.start()
        sent.append(copy)

    def collect(i):
        arrived(slot(peers[i], core_w))
        arrived(slot(peers[i], far_w))

    own_rows = pl.ds(pl.multiple_of(y * pack, pack), pack)
    other_rows = pl.ds(pl.multiple_of(other_y * pack, pack), pack)

    def y_copy(c, t):
        return pltpu.make_async_remote_copy(
            src_ref=y_out.at[c, t], dst_ref=y_in.at[c, t],
            send_sem=y_send.at[c, t], recv_sem=y_recv.at[c, t],
            device_id=(z * 2 + other_y, me_w), device_id_type=MESH,
        )

    def near_copy(j, t):
        return pltpu.make_async_remote_copy(
            src_ref=near_out.at[j, t], dst_ref=near_in.at[j, t],
            send_sem=near_send.at[j, t], recv_sem=near_recv.at[j, t],
            device_id=(near_z * 2 + y, me_w), device_id_type=MESH,
        )

    def kv_copy(j):
        return pltpu.make_async_remote_copy(
            src_ref=kv_out.at[j], dst_ref=kv_in.at[j],
            send_sem=kv_send.at[j], recv_sem=kv_recv.at[j],
            device_id=(near_z * 2 + y, me_w), device_id_type=MESH,
        )

    def mid_copy(t):
        return pltpu.make_async_remote_copy(
            src_ref=mid_out.at[t], dst_ref=mid_in.at[t],
            send_sem=mid_send.at[t], recv_sem=mid_recv.at[t],
            device_id=(mid_z * 2 + y, me_w), device_id_type=MESH,
        )

    def chunk(c):
        return pl.ds(pl.multiple_of(order[c] * 2 * pack, 2 * pack), 2 * pack)

    def product(c, t):
        return jnp.dot(rows[chunk(c), :], weights[t], preferred_element_type=jnp.float32)

    def multiply_kv(c):
        if c % 2:
            kv_out[c // 2] = product(c, q_tiles).astype(jnp.bfloat16)
            kv_copy(c // 2).start()
        else:
            own[c, q_tiles] = product(c, q_tiles)

    def multiply(c, start):
        @pl.loop(0, q_tiles)
        def _(t):
            own[c, t] = product(c, t)
            y_out[c, t] = own[c, t, other_rows, :].astype(jnp.bfloat16)
            if start:
                y_copy(c, t).start()

    def pair_sum(c, t):
        y_copy(c, t).wait_recv()
        return own[c, t, own_rows, :] + y_in[c, t].astype(jnp.float32)

    def pass_near(j, start_next):
        @pl.loop(0, q_tiles)
        def _(t):
            total = pair_sum(2 * j + 1, t)
            if start_next:
                y_copy(2, t).start()
            near_out[j, t] = total.astype(jnp.bfloat16)
            near_copy(j, t).start()

    def ready(*chunks):
        for step in (forward, relay, collect):
            for c in chunks:
                step(2 * c)
                step(2 * c + 1)

    ready(0)
    for load in loads:
        load.wait()
    multiply(0, True)
    ready(1)
    multiply_kv(1)
    multiply(1, True)
    ready(2, 3)
    multiply_kv(3)
    multiply(2, False)
    multiply_kv(2)
    multiply_kv(0)
    pass_near(0, True)
    multiply(3, False)
    for c, j in ((2, 0), (0, 1)):
        kv_copy(j).wait_recv()
        own[c, q_tiles] = own[c, q_tiles] + kv_in[j].astype(jnp.float32)
        y_out[c, q_tiles] = own[c, q_tiles, other_rows, :].astype(jnp.bfloat16)

    y_later = [(2, q_tiles), (0, q_tiles)] + [(3, t) for t in range(q_tiles)]
    for t in range(q_tiles):
        total = pair_sum(2, t)
        y_copy(*y_later[t]).start()
        near_copy(0, t).wait_recv()
        mid_out[t] = (total + near_in[0, t].astype(jnp.float32)).astype(jnp.bfloat16)
        mid_copy(t).start()

    mid_out[q_tiles] = pair_sum(2, q_tiles).astype(jnp.bfloat16)
    mid_copy(q_tiles).start()
    for later in y_later[q_tiles:]:
        y_copy(*later).start()
    pass_near(1, False)

    def rope(head):
        return head * cosine_ref[...] + pltpu.roll(head, HEAD_DIM // 2, 1) * sine_ref[...]

    kv_total = pair_sum(0, q_tiles)
    mid_copy(q_tiles).wait_recv()
    kv_total = (kv_total + mid_in[q_tiles].astype(jnp.float32)).astype(jnp.bfloat16)
    kv_heads = kv // HEAD_DIM
    for h in range(kv_heads):
        first_col = h * HEAD_DIM
        key_head = kv_total[:, first_col : first_col + HEAD_DIM].astype(jnp.float32)
        held_keys[h] = rope(key_head).astype(jnp.bfloat16)
        held_values[h] = kv_total[:, kv + first_col : kv + first_col + HEAD_DIM]

    places_i = lax.broadcasted_iota(jnp.int32, (pack, pack), 0)
    places_j = lax.broadcasted_iota(jnp.int32, (pack, pack), 1)
    allowed = (seg_col_ref[...] == seg_row_ref[...]) & (places_j <= places_i)

    @pl.loop(0, q_tiles)
    def _(t):
        total = pair_sum(0, t)
        mid_copy(t).wait_recv()
        total = total + mid_in[t].astype(jnp.float32)
        near_copy(1, t).wait_recv()
        total = total + near_in[1, t].astype(jnp.float32)
        kv_head = t * kv_heads // q_tiles
        keys, values = held_keys[kv_head], held_values[kv_head]
        mixed = []
        for h in range(TILE // HEAD_DIM):
            head = rope(total[:, h * HEAD_DIM : (h + 1) * HEAD_DIM]).astype(jnp.bfloat16)
            scores = lax.dot_general(
                head, keys, (((1,), (1,)), ((), ())), preferred_element_type=jnp.float32
            ) * HEAD_DIM ** (-0.5)
            chances = jnp.where(allowed, jnp.exp(scores), 0.0)
            chances = chances * (1.0 / jnp.sum(chances, axis=1, keepdims=True))
            mixed.append(
                jnp.dot(chances.astype(jnp.bfloat16), values, preferred_element_type=jnp.float32)
            )
        columns = pl.ds(pl.multiple_of(t * TILE, TILE), TILE)
        out_ref[:, columns] = jnp.concatenate(mixed, axis=1).astype(jnp.bfloat16)

    for copy in sent:
        copy.wait_send()

    @pl.loop(0, q_tiles)
    def _(t):
        for c in range(4):
            y_copy(c, t).wait_send()
        for j in range(2):
            near_copy(j, t).wait_send()
        mid_copy(t).wait_send()

    for j in range(2):
        kv_copy(j).wait_send()
        y_copy(2 * j, q_tiles).wait_send()
    mid_copy(q_tiles).wait_send()


def attend_on_slice(tokens, segment_ids, norm_gain, query_weight, key_weight, value_weight):
    count, features = tokens.shape
    slab, query_cols = query_weight.shape
    tiles = query_cols // TILE + 1
    pack = 4 * count
    cosine, sine_part = rope_tables(positions_in_segment(segment_ids), HEAD_DIM)
    bf16, f32 = jnp.bfloat16, jnp.float32
    dma = pltpu.SemaphoreType.DMA
    vmem = pl.BlockSpec(memory_space=pltpu.VMEM)
    hbm = pl.BlockSpec(memory_space=pltpu.HBM)
    return pl.pallas_call(
        attend_kernel,
        out_shape=jax.ShapeDtypeStruct((pack, query_cols), bf16),
        in_specs=[hbm] * 5 + [vmem] * 4,
        out_specs=vmem,
        scratch_shapes=[
            pltpu.VMEM((count, features), bf16),
            pltpu.VMEM((1, features), f32),
            pltpu.VMEM((tiles, slab, TILE), bf16),
            pltpu.VMEM((8, count, slab), bf16),
            pltpu.VMEM((8 * pack, slab), bf16),
            pltpu.VMEM((4, tiles, 2 * pack, TILE), f32),
            pltpu.VMEM((4, tiles, pack, TILE), bf16),
            pltpu.VMEM((4, tiles, pack, TILE), bf16),
            pltpu.VMEM((2, tiles - 1, pack, TILE), bf16),
            pltpu.VMEM((2, tiles - 1, pack, TILE), bf16),
            pltpu.VMEM((2, 2 * pack, TILE), bf16),
            pltpu.VMEM((2, 2 * pack, TILE), bf16),
            pltpu.VMEM((tiles, pack, TILE), bf16),
            pltpu.VMEM((tiles, pack, TILE), bf16),
            pltpu.VMEM((TILE // 2 // HEAD_DIM, pack, HEAD_DIM), bf16),
            pltpu.VMEM((TILE // 2 // HEAD_DIM, pack, HEAD_DIM), bf16),
            dma((tiles + 3,)),
            dma((8,)),
            dma((32,)),
            dma((8,)),
            dma((8,)),
            dma((8,)),
            dma((4, tiles)),
            dma((4, tiles)),
            dma((2, tiles - 1)),
            dma((2, tiles - 1)),
            dma((2,)),
            dma((2,)),
            dma((tiles,)),
            dma((tiles,)),
        ],
        compiler_params=pltpu.CompilerParams(
            collective_id=0, has_side_effects=True, vmem_limit_bytes=56 * 1024 * 1024
        ),
        cost_estimate=pl.CostEstimate(
            flops=2 * 8 * pack * slab * tiles * TILE, bytes_accessed=2 * slab * tiles * TILE, transcendentals=0
        ),
    )(
        tokens, norm_gain[None, :], query_weight, key_weight, value_weight,
        jnp.concatenate([cosine, cosine], axis=1), jnp.concatenate([-sine_part, sine_part], axis=1),
        segment_ids[:, None], segment_ids[None, :],
    )


def per_device(tokens, segment_ids, norm_gain, query_weight, key_weight, value_weight):
    head_dim = HEAD_DIM
    query_cols = query_weight.shape[1]
    heads_dev = query_cols // head_dim
    group_size = HEADS // KV_HEADS
    local_kv = max(1, heads_dev // group_size)
    first_kv = lax.axis_index("weight") * heads_dev // group_size
    key_width = local_kv * head_dim
    if (lax.axis_size("batch"), lax.axis_size("weight"), 2 * key_width) == (8, 4, TILE):
        return attend_on_slice(tokens, segment_ids, norm_gain, query_weight, key_weight, value_weight)
    key_block = lax.dynamic_slice_in_dim(key_weight, first_kv * head_dim, key_width, 1)
    value_block = lax.dynamic_slice_in_dim(value_weight, first_kv * head_dim, key_width, 1)
    values = tokens.astype(jnp.float32)
    inverse_rms = lax.rsqrt(jnp.mean(values * values, axis=1, keepdims=True) + EPSILON)
    normed = (values * inverse_rms * norm_gain[None, :]).astype(jnp.bfloat16)
    local_weights = jnp.concatenate([query_weight, key_block, value_block], axis=1)
    full_weights = lax.all_gather(local_weights, "batch", axis=0, tiled=True)
    projected = jnp.dot(
        lax.all_gather(normed, "weight", axis=0, tiled=True),
        full_weights,
        preferred_element_type=jnp.float32,
    )
    query_part = projected[:, :query_cols]
    key_rows = projected[:, query_cols : query_cols + key_width].astype(jnp.bfloat16)
    value_rows = projected[:, query_cols + key_width :].astype(jnp.bfloat16)
    pack_rows = segment_ids.shape[0]
    positions = positions_in_segment(segment_ids)
    queries = rotate(query_part.reshape(pack_rows, heads_dev, head_dim), positions).astype(
        jnp.bfloat16
    )
    rotated_keys = rotate(
        key_rows.astype(jnp.float32).reshape(pack_rows, local_kv, head_dim), positions
    ).astype(jnp.bfloat16)
    grouped = queries.reshape(pack_rows, local_kv, heads_dev // local_kv, head_dim)
    attended = attend(
        grouped, rotated_keys, value_rows.reshape(pack_rows, local_kv, head_dim), segment_ids
    )
    return attended.reshape(pack_rows, query_cols)


def solution(mesh):
    placed = (
        P(("batch", "weight"), None),
        P("batch"),
        P(),
        P("batch", "weight"),
        P("batch", None),
        P("batch", None),
    )
    return jax.shard_map(
        per_device, mesh=mesh, in_specs=placed, out_specs=P("batch", "weight"), check_vma=False
    )
```

```python
import math

import jax
import jax.numpy as jnp
from jax import lax
from jax.experimental import pallas as pl
from jax.experimental.pallas import tpu as pltpu
from jax.sharding import PartitionSpec as P

HEADS = 64
KV_HEADS = 8
HEAD_DIM = 128


ROPE_BASE = 500000.0
EPSILON = 1e-05


def positions_in_segment(seg_ids):
    places = jnp.arange(seg_ids.shape[0], dtype=jnp.int32)
    earlier = jnp.concatenate([seg_ids[:1] - 1, seg_ids[:-1]])
    starts = jnp.where(seg_ids != earlier, places, 0)
    leading = lax.cummax(starts, axis=0)
    return places - leading


def rope_tables(positions, head_dim):
    ratios = jnp.arange(head_dim // 2, dtype=jnp.float32) * (2.0 / head_dim)
    frequency = jnp.exp(-math.log(ROPE_BASE) * ratios)
    angles = positions.astype(jnp.float32)[:, None] * frequency[None, :]
    return jnp.cos(angles), jnp.sin(angles)


def rotate(vectors, positions):
    half_dim = vectors.shape[-1] // 2
    cosine, sine_part = rope_tables(positions, vectors.shape[-1])
    cosine, sine_part = cosine[:, None, :], sine_part[:, None, :]
    front_half = vectors[..., :half_dim]
    back_half = vectors[..., half_dim:]
    return jnp.concatenate(
        [front_half * cosine - back_half * sine_part, back_half * cosine + front_half * sine_part],
        axis=-1,
    )


def attend(grouped, rotated_keys, value_rows, seg_ids):
    scores = jnp.einsum(
        "ingd,jnd->ngij", grouped, rotated_keys, preferred_element_type=jnp.float32
    ) * grouped.shape[-1] ** (-0.5)
    places = jnp.arange(seg_ids.shape[0], dtype=jnp.int32)
    allowed = (seg_ids[:, None] == seg_ids[None, :]) & (places[None, :] <= places[:, None])
    weights = jnp.where(allowed, jnp.exp(scores), 0.0)
    probabilities = (weights / jnp.sum(weights, axis=-1, keepdims=True)).astype(jnp.bfloat16)
    mixed = jnp.einsum(
        "ngij,jnd->ingd", probabilities, value_rows, preferred_element_type=jnp.float32
    )
    return mixed.astype(jnp.bfloat16)


MESH = pl.DeviceIdType.MESH
TILE = 512


def attend_kernel(
    tokens_ref, gain_ref, query_ref, key_ref, value_ref, seg_ref, out_ref,
    tokens, gain, weights, normed, rows, own, y_out, y_in, near_out, near_in, kv_out, kv_in, mid_out, mid_in, held_keys, held_values, cosine, sine, allowed,
    load_sem, tok_send, tok_recv, x_send, core_send, relay_send,
    y_send, y_recv, near_send, near_recv, kv_send, kv_recv, mid_send, mid_recv,
):
    me_b = lax.axis_index("batch")
    me_w = lax.axis_index("weight")
    z, y = me_b // 2, me_b % 2
    count, features = tokens_ref.shape
    slab = query_ref.shape[0]
    pack = 4 * count
    tiles = weights.shape[0]
    q_tiles = tiles - 1
    kv = TILE // 2

    near_z, mid_z = z + 1 - 2 * (z % 2), (z + 2) % 4
    order = [z, 3 - z, mid_z, near_z]
    other_y = 1 - y
    sources = [(zz * 2 + y, zz * 2 + other_y) for zz in order]
    peers = [b for pair in sources for b in pair]
    x_w, core_w, far_w = (me_w + 2) % 4, me_w + 1 - 2 * (me_w % 2), 3 - me_w

    barrier = pltpu.get_barrier_semaphore()
    for i, b in enumerate(peers):
        if i != 0:
            pl.semaphore_signal(barrier, inc=1, device_id=(b, me_w), device_id_type=MESH)
    for w in (x_w, core_w):
        pl.semaphore_signal(barrier, inc=1, device_id=(me_b, w), device_id_type=MESH)

    token_load = pltpu.make_async_copy(tokens_ref, tokens, load_sem.at[tiles + 1])
    gain_load = pltpu.make_async_copy(gain_ref, gain, load_sem.at[tiles + 2])
    token_load.start()
    gain_load.start()
    loads = [
        pltpu.make_async_copy(
            query_ref.at[:, pl.ds(t * TILE, TILE)], weights.at[t], load_sem.at[t]
        )
        for t in range(q_tiles)
    ]
    first = pl.ds(pl.multiple_of(me_w * kv, kv), kv)
    loads.append(
        pltpu.make_async_copy(
            key_ref.at[:, first], weights.at[q_tiles, :, pl.ds(0, kv)], load_sem.at[q_tiles]
        )
    )
    loads.append(
        pltpu.make_async_copy(
            value_ref.at[:, first], weights.at[q_tiles, :, pl.ds(kv, kv)], load_sem.at[tiles]
        )
    )
    for load in loads:
        load.start()

    token_load.wait()
    gain_load.wait()
    total = jnp.zeros((count, 1), jnp.float32)
    for k in range(features // slab):
        part = tokens[:, k * slab : (k + 1) * slab].astype(jnp.float32)
        total = total + jnp.sum(part * part, axis=1, keepdims=True)
    inverse_rms = lax.rsqrt(total * (1.0 / features) + EPSILON)
    for k in range(features // slab):
        part = tokens[:, k * slab : (k + 1) * slab].astype(jnp.float32)
        normed[k] = (part * inverse_rms * gain[:, k * slab : (k + 1) * slab]).astype(jnp.bfloat16)

    def slot(b, w):
        return b * 4 + w

    def at_slot(s):
        return rows.at[pl.ds(pl.multiple_of(s * count, count), count)]

    def send(src, s, device, send_sem):
        return pltpu.make_async_remote_copy(
            src_ref=src, dst_ref=at_slot(s), send_sem=send_sem, recv_sem=tok_recv.at[s],
            device_id=device, device_id_type=MESH,
        )

    def arrived(s):
        send(at_slot(s), s, (me_b, x_w), x_send.at[0]).wait_recv()

    pl.semaphore_wait(barrier, 9)
    mine = slot(me_b, me_w)
    sent = []
    for i, b in enumerate(peers):
        if i != 0:
            copy = send(normed.at[b], mine, (b, me_w), tok_send.at[i])
            copy.start()
            sent.append(copy)
    rows[pl.ds(pl.multiple_of(mine * count, count), count), :] = normed[me_b]

    def forward(i):
        b = peers[i]
        s = slot(b, me_w)
        if i != 0:
            arrived(s)
        for w, sem in ((x_w, x_send), (core_w, core_send)):
            copy = send(at_slot(s), s, (me_b, w), sem.at[i])
            copy.start()
            sent.append(copy)

    def relay(i):
        s = slot(peers[i], x_w)
        arrived(s)
        copy = send(at_slot(s), s, (me_b, core_w), relay_send.at[i])
        copy.start()
        sent.append(copy)

    def collect(i):
        arrived(slot(peers[i], core_w))
        arrived(slot(peers[i], far_w))

    own_rows = pl.ds(pl.multiple_of(y * pack, pack), pack)
    other_rows = pl.ds(pl.multiple_of(other_y * pack, pack), pack)

    def y_copy(c, t):
        return pltpu.make_async_remote_copy(
            src_ref=y_out.at[c, t], dst_ref=y_in.at[c, t],
            send_sem=y_send.at[c, t], recv_sem=y_recv.at[c, t],
            device_id=(z * 2 + other_y, me_w), device_id_type=MESH,
        )

    def near_copy(j, t):
        return pltpu.make_async_remote_copy(
            src_ref=near_out.at[j, t], dst_ref=near_in.at[j, t],
            send_sem=near_send.at[j, t], recv_sem=near_recv.at[j, t],
            device_id=(near_z * 2 + y, me_w), device_id_type=MESH,
        )

    def kv_copy(j):
        return pltpu.make_async_remote_copy(
            src_ref=kv_out.at[j], dst_ref=kv_in.at[j],
            send_sem=kv_send.at[j], recv_sem=kv_recv.at[j],
            device_id=(near_z * 2 + y, me_w), device_id_type=MESH,
        )

    def mid_copy(t):
        return pltpu.make_async_remote_copy(
            src_ref=mid_out.at[t], dst_ref=mid_in.at[t],
            send_sem=mid_send.at[t], recv_sem=mid_recv.at[t],
            device_id=(mid_z * 2 + y, me_w), device_id_type=MESH,
        )

    def chunk(c):
        return pl.ds(pl.multiple_of(order[c] * 2 * pack, 2 * pack), 2 * pack)

    def product(c, t):
        return jnp.dot(rows[chunk(c), :], weights[t], preferred_element_type=jnp.float32)

    def multiply_kv(c):
        if c % 2:
            kv_out[c // 2] = product(c, q_tiles).astype(jnp.bfloat16)
            kv_copy(c // 2).start()
        else:
            own[c, q_tiles] = product(c, q_tiles)

    def make_tables():
        places_i = lax.broadcasted_iota(jnp.int32, (pack, pack), 0)
        places_j = lax.broadcasted_iota(jnp.int32, (pack, pack), 1)
        seg_j = jnp.broadcast_to(seg_ref[...], (pack, pack))
        same = seg_j.T == seg_j
        allowed[...] = jnp.where(same & (places_j <= places_i), 1.0, 0.0)
        start = jnp.min(jnp.where(same, places_j, pack).astype(jnp.float32), axis=1, keepdims=True)
        shape = (pack, HEAD_DIM)
        position = lax.broadcasted_iota(jnp.int32, shape, 0).astype(jnp.float32) - start
        lane = lax.broadcasted_iota(jnp.int32, shape, 1)
        half_dim = HEAD_DIM // 2
        ratio = (lane % half_dim).astype(jnp.float32) * (2.0 / HEAD_DIM)
        angles = position * jnp.exp(-math.log(ROPE_BASE) * ratio)
        cosine[...] = jnp.cos(angles)
        sine[...] = jnp.where(lane < half_dim, -1.0, 1.0) * jnp.sin(angles)

    def multiply(c, start, first_tile=0, last_tile=q_tiles):
        @pl.loop(first_tile, last_tile)
        def _(t):
            own[c, t] = product(c, t)
            y_out[c, t] = own[c, t, other_rows, :].astype(jnp.bfloat16)
            if start:
                y_copy(c, t).start()

    def pair_sum(c, t):
        y_copy(c, t).wait_recv()
        return own[c, t, own_rows, :] + y_in[c, t].astype(jnp.float32)

    def pass_near(j, y_next):
        for t in range(q_tiles):
            total = pair_sum(2 * j + 1, t)
            if t < len(y_next):
                y_copy(*y_next[t]).start()
            near_out[j, t] = total.astype(jnp.bfloat16)
            near_copy(j, t).start()

    def ready(*chunks):
        for step in (forward, relay, collect):
            for c in chunks:
                step(2 * c)
                step(2 * c + 1)

    ready(0)
    for load in loads:
        load.wait()
    multiply(0, True, 0, q_tiles - 1)
    ready(1)
    multiply(1, True)
    multiply_kv(1)
    ready(2, 3)
    multiply_kv(3)
    multiply(2, False)
    multiply_kv(2)
    multiply_kv(0)
    make_tables()
    pass_near(0, [(2, t) for t in range(q_tiles)])
    multiply(3, False)
    multiply(0, False, q_tiles - 1)
    for c, j in ((2, 0), (0, 1)):
        kv_copy(j).wait_recv()
        own[c, q_tiles] = own[c, q_tiles] + kv_in[j].astype(jnp.float32)
        y_out[c, q_tiles] = own[c, q_tiles, other_rows, :].astype(jnp.bfloat16)

    y_later = [(2, q_tiles), (0, q_tiles)] + [(3, t) for t in range(q_tiles)]
    for t in range(q_tiles):
        total = pair_sum(2, t)
        y_copy(*y_later[t]).start()
        near_copy(0, t).wait_recv()
        mid_out[t] = (total + near_in[0, t].astype(jnp.float32)).astype(jnp.bfloat16)
        mid_copy(t).start()

    mid_out[q_tiles] = pair_sum(2, q_tiles).astype(jnp.bfloat16)
    mid_copy(q_tiles).start()
    for later in y_later[q_tiles:]:
        y_copy(*later).start()
    pass_near(1, [(0, q_tiles - 1)])

    def rope(head):
        return head * cosine[...] + pltpu.roll(head, HEAD_DIM // 2, 1) * sine[...]

    kv_total = pair_sum(0, q_tiles)
    mid_copy(q_tiles).wait_recv()
    kv_total = (kv_total + mid_in[q_tiles].astype(jnp.float32)).astype(jnp.bfloat16)
    kv_heads = kv // HEAD_DIM
    for h in range(kv_heads):
        first_col = h * HEAD_DIM
        key_head = kv_total[:, first_col : first_col + HEAD_DIM].astype(jnp.float32)
        held_keys[h] = rope(key_head).astype(jnp.bfloat16)
        held_values[h] = kv_total[:, kv + first_col : kv + first_col + HEAD_DIM]

    @pl.loop(0, q_tiles)
    def _(t):
        total = pair_sum(0, t)
        mid_copy(t).wait_recv()
        total = total + mid_in[t].astype(jnp.float32)
        near_copy(1, t).wait_recv()
        total = total + near_in[1, t].astype(jnp.float32)
        kv_head = t * kv_heads // q_tiles
        keys, values = held_keys[kv_head], held_values[kv_head]
        mixed = []
        for h in range(TILE // HEAD_DIM):
            head = rope(total[:, h * HEAD_DIM : (h + 1) * HEAD_DIM]).astype(jnp.bfloat16)
            scores = lax.dot_general(
                head, keys, (((1,), (1,)), ((), ())), preferred_element_type=jnp.float32
            ) * HEAD_DIM ** (-0.5)
            chances = jnp.where(allowed[...] > 0.0, jnp.exp(scores), 0.0)
            chances = chances * (1.0 / jnp.sum(chances, axis=1, keepdims=True))
            mixed.append(
                jnp.dot(chances.astype(jnp.bfloat16), values, preferred_element_type=jnp.float32)
            )
        columns = pl.ds(pl.multiple_of(t * TILE, TILE), TILE)
        out_ref[:, columns] = jnp.concatenate(mixed, axis=1).astype(jnp.bfloat16)

    for copy in sent:
        copy.wait_send()

    @pl.loop(0, q_tiles)
    def _(t):
        for c in range(4):
            y_copy(c, t).wait_send()
        for j in range(2):
            near_copy(j, t).wait_send()
        mid_copy(t).wait_send()

    for j in range(2):
        kv_copy(j).wait_send()
        y_copy(2 * j, q_tiles).wait_send()
    mid_copy(q_tiles).wait_send()


def attend_on_slice(tokens, segment_ids, norm_gain, query_weight, key_weight, value_weight):
    count, features = tokens.shape
    slab, query_cols = query_weight.shape
    tiles = query_cols // TILE + 1
    pack = 4 * count
    bf16, f32 = jnp.bfloat16, jnp.float32
    dma = pltpu.SemaphoreType.DMA
    vmem = pl.BlockSpec(memory_space=pltpu.VMEM)
    hbm = pl.BlockSpec(memory_space=pltpu.HBM)
    return pl.pallas_call(
        attend_kernel,
        out_shape=jax.ShapeDtypeStruct((pack, query_cols), bf16),
        in_specs=[hbm] * 5 + [vmem],
        out_specs=vmem,
        scratch_shapes=[
            pltpu.VMEM((count, features), bf16),
            pltpu.VMEM((1, features), f32),
            pltpu.VMEM((tiles, slab, TILE), bf16),
            pltpu.VMEM((8, count, slab), bf16),
            pltpu.VMEM((8 * pack, slab), bf16),
            pltpu.VMEM((4, tiles, 2 * pack, TILE), f32),
            pltpu.VMEM((4, tiles, pack, TILE), bf16),
            pltpu.VMEM((4, tiles, pack, TILE), bf16),
            pltpu.VMEM((2, tiles - 1, pack, TILE), bf16),
            pltpu.VMEM((2, tiles - 1, pack, TILE), bf16),
            pltpu.VMEM((2, 2 * pack, TILE), bf16),
            pltpu.VMEM((2, 2 * pack, TILE), bf16),
            pltpu.VMEM((tiles, pack, TILE), bf16),
            pltpu.VMEM((tiles, pack, TILE), bf16),
            pltpu.VMEM((TILE // 2 // HEAD_DIM, pack, HEAD_DIM), bf16),
            pltpu.VMEM((TILE // 2 // HEAD_DIM, pack, HEAD_DIM), bf16),
            pltpu.VMEM((pack, HEAD_DIM), f32),
            pltpu.VMEM((pack, HEAD_DIM), f32),
            pltpu.VMEM((pack, pack), f32),
            dma((tiles + 3,)),
            dma((8,)),
            dma((32,)),
            dma((8,)),
            dma((8,)),
            dma((8,)),
            dma((4, tiles)),
            dma((4, tiles)),
            dma((2, tiles - 1)),
            dma((2, tiles - 1)),
            dma((2,)),
            dma((2,)),
            dma((tiles,)),
            dma((tiles,)),
        ],
        compiler_params=pltpu.CompilerParams(
            collective_id=0, has_side_effects=True, vmem_limit_bytes=53 * 1024 * 1024
        ),
        cost_estimate=pl.CostEstimate(
            flops=2 * 8 * pack * slab * tiles * TILE, bytes_accessed=2 * slab * tiles * TILE, transcendentals=0
        ),
    )(
        tokens, norm_gain[None, :], query_weight, key_weight, value_weight,
        segment_ids[None, :],
    )


def per_device(tokens, segment_ids, norm_gain, query_weight, key_weight, value_weight):
    head_dim = HEAD_DIM
    query_cols = query_weight.shape[1]
    heads_dev = query_cols // head_dim
    group_size = HEADS // KV_HEADS
    local_kv = max(1, heads_dev // group_size)
    first_kv = lax.axis_index("weight") * heads_dev // group_size
    key_width = local_kv * head_dim
    if (lax.axis_size("batch"), lax.axis_size("weight"), 2 * key_width) == (8, 4, TILE):
        return attend_on_slice(tokens, segment_ids, norm_gain, query_weight, key_weight, value_weight)
    key_block = lax.dynamic_slice_in_dim(key_weight, first_kv * head_dim, key_width, 1)
    value_block = lax.dynamic_slice_in_dim(value_weight, first_kv * head_dim, key_width, 1)
    values = tokens.astype(jnp.float32)
    inverse_rms = lax.rsqrt(jnp.mean(values * values, axis=1, keepdims=True) + EPSILON)
    normed = (values * inverse_rms * norm_gain[None, :]).astype(jnp.bfloat16)
    local_weights = jnp.concatenate([query_weight, key_block, value_block], axis=1)
    full_weights = lax.all_gather(local_weights, "batch", axis=0, tiled=True)
    projected = jnp.dot(
        lax.all_gather(normed, "weight", axis=0, tiled=True),
        full_weights,
        preferred_element_type=jnp.float32,
    )
    query_part = projected[:, :query_cols]
    key_rows = projected[:, query_cols : query_cols + key_width].astype(jnp.bfloat16)
    value_rows = projected[:, query_cols + key_width :].astype(jnp.bfloat16)
    pack_rows = segment_ids.shape[0]
    positions = positions_in_segment(segment_ids)
    queries = rotate(query_part.reshape(pack_rows, heads_dev, head_dim), positions).astype(
        jnp.bfloat16
    )
    rotated_keys = rotate(
        key_rows.astype(jnp.float32).reshape(pack_rows, local_kv, head_dim), positions
    ).astype(jnp.bfloat16)
    grouped = queries.reshape(pack_rows, local_kv, heads_dev // local_kv, head_dim)
    attended = attend(
        grouped, rotated_keys, value_rows.reshape(pack_rows, local_kv, head_dim), segment_ids
    )
    return attended.reshape(pack_rows, query_cols)


def solution(mesh):
    placed = (
        P(("batch", "weight"), None),
        P("batch"),
        P(),
        P("batch", "weight"),
        P("batch", None),
        P("batch", None),
    )
    return jax.shard_map(
        per_device, mesh=mesh, in_specs=placed, out_specs=P("batch", "weight"), check_vma=False
    )
```

```python
import math

import jax
import jax.numpy as jnp
from jax import lax
from jax.experimental import pallas as pl
from jax.experimental.pallas import tpu as pltpu
from jax.sharding import PartitionSpec as P

HEADS = 64
KV_HEADS = 8
HEAD_DIM = 128


ROPE_BASE = 500000.0
EPSILON = 1e-05


def positions_in_segment(seg_ids):
    places = jnp.arange(seg_ids.shape[0], dtype=jnp.int32)
    earlier = jnp.concatenate([seg_ids[:1] - 1, seg_ids[:-1]])
    starts = jnp.where(seg_ids != earlier, places, 0)
    leading = lax.cummax(starts, axis=0)
    return places - leading


def rope_tables(positions, head_dim):
    ratios = jnp.arange(head_dim // 2, dtype=jnp.float32) * (2.0 / head_dim)
    frequency = jnp.exp(-math.log(ROPE_BASE) * ratios)
    angles = positions.astype(jnp.float32)[:, None] * frequency[None, :]
    return jnp.cos(angles), jnp.sin(angles)


def rotate(vectors, positions):
    half_dim = vectors.shape[-1] // 2
    cosine, sine_part = rope_tables(positions, vectors.shape[-1])
    cosine, sine_part = cosine[:, None, :], sine_part[:, None, :]
    front_half = vectors[..., :half_dim]
    back_half = vectors[..., half_dim:]
    return jnp.concatenate(
        [front_half * cosine - back_half * sine_part, back_half * cosine + front_half * sine_part],
        axis=-1,
    )


def attend(grouped, rotated_keys, value_rows, seg_ids):
    scores = jnp.einsum(
        "ingd,jnd->ngij", grouped, rotated_keys, preferred_element_type=jnp.float32
    ) * grouped.shape[-1] ** (-0.5)
    places = jnp.arange(seg_ids.shape[0], dtype=jnp.int32)
    allowed = (seg_ids[:, None] == seg_ids[None, :]) & (places[None, :] <= places[:, None])
    weights = jnp.where(allowed, jnp.exp(scores), 0.0)
    probabilities = (weights / jnp.sum(weights, axis=-1, keepdims=True)).astype(jnp.bfloat16)
    mixed = jnp.einsum(
        "ngij,jnd->ingd", probabilities, value_rows, preferred_element_type=jnp.float32
    )
    return mixed.astype(jnp.bfloat16)


MESH = pl.DeviceIdType.MESH
TILE = 512


def attend_kernel(
    tokens_ref, gain_ref, query_ref, key_ref, value_ref, seg_ref, out_ref,
    tokens, gain, weights, normed, rows, own, y_out, y_in, near_out, near_in, kv_out, kv_in, mid_out, mid_in, held_keys, held_values, cosine, sine, allowed,
    load_sem, tok_send, tok_recv, x_send, core_send, relay_send,
    y_send, y_recv, near_send, near_recv, kv_send, kv_recv, mid_send, mid_recv,
):
    me_b = lax.axis_index("batch")
    me_w = lax.axis_index("weight")
    z, y = me_b // 2, me_b % 2
    count, features = tokens_ref.shape
    slab = query_ref.shape[0]
    pack = 4 * count
    tiles = weights.shape[0]
    q_tiles = tiles - 1
    kv = TILE // 2

    near_z, mid_z = z + 1 - 2 * (z % 2), (z + 2) % 4
    order = [z, 3 - z, mid_z, near_z]
    other_y = 1 - y
    sources = [(zz * 2 + y, zz * 2 + other_y) for zz in order]
    peers = [b for pair in sources for b in pair]
    x_w, core_w, far_w = (me_w + 2) % 4, me_w + 1 - 2 * (me_w % 2), 3 - me_w

    barrier = pltpu.get_barrier_semaphore()
    for i, b in enumerate(peers):
        if i != 0:
            pl.semaphore_signal(barrier, inc=1, device_id=(b, me_w), device_id_type=MESH)
    for w in (x_w, core_w):
        pl.semaphore_signal(barrier, inc=1, device_id=(me_b, w), device_id_type=MESH)

    token_load = pltpu.make_async_copy(tokens_ref, tokens, load_sem.at[tiles + 1])
    gain_load = pltpu.make_async_copy(gain_ref, gain, load_sem.at[tiles + 2])
    token_load.start()
    gain_load.start()
    loads = [
        pltpu.make_async_copy(
            query_ref.at[:, pl.ds(t * TILE, TILE)], weights.at[t], load_sem.at[t]
        )
        for t in range(q_tiles)
    ]
    first = pl.ds(pl.multiple_of(me_w * kv, kv), kv)
    loads.append(
        pltpu.make_async_copy(
            key_ref.at[:, first], weights.at[q_tiles, :, pl.ds(0, kv)], load_sem.at[q_tiles]
        )
    )
    loads.append(
        pltpu.make_async_copy(
            value_ref.at[:, first], weights.at[q_tiles, :, pl.ds(kv, kv)], load_sem.at[tiles]
        )
    )
    for load in loads:
        load.start()

    token_load.wait()
    gain_load.wait()
    total = jnp.zeros((count, 1), jnp.float32)
    for k in range(features // slab):
        part = tokens[:, k * slab : (k + 1) * slab].astype(jnp.float32)
        total = total + jnp.sum(part * part, axis=1, keepdims=True)
    inverse_rms = lax.rsqrt(total * (1.0 / features) + EPSILON)
    for k in range(features // slab):
        part = tokens[:, k * slab : (k + 1) * slab].astype(jnp.float32)
        normed[k] = (part * inverse_rms * gain[:, k * slab : (k + 1) * slab]).astype(jnp.bfloat16)

    def slot(b, w):
        return b * 4 + w

    def at_slot(s):
        return rows.at[pl.ds(pl.multiple_of(s * count, count), count)]

    def send(src, s, device, send_sem):
        return pltpu.make_async_remote_copy(
            src_ref=src, dst_ref=at_slot(s), send_sem=send_sem, recv_sem=tok_recv.at[s],
            device_id=device, device_id_type=MESH,
        )

    def arrived(s):
        send(at_slot(s), s, (me_b, x_w), x_send.at[0]).wait_recv()

    pl.semaphore_wait(barrier, 9)
    mine = slot(me_b, me_w)
    sent = []
    for i, b in enumerate(peers):
        if i != 0:
            copy = send(normed.at[b], mine, (b, me_w), tok_send.at[i])
            copy.start()
            sent.append(copy)
    rows[pl.ds(pl.multiple_of(mine * count, count), count), :] = normed[me_b]

    def forward(i):
        b = peers[i]
        s = slot(b, me_w)
        if i != 0:
            arrived(s)
        for w, sem in ((x_w, x_send), (core_w, core_send)):
            copy = send(at_slot(s), s, (me_b, w), sem.at[i])
            copy.start()
            sent.append(copy)

    def relay(i):
        s = slot(peers[i], x_w)
        arrived(s)
        copy = send(at_slot(s), s, (me_b, core_w), relay_send.at[i])
        copy.start()
        sent.append(copy)

    def collect(i):
        arrived(slot(peers[i], core_w))
        arrived(slot(peers[i], far_w))

    own_rows = pl.ds(pl.multiple_of(y * pack, pack), pack)
    other_rows = pl.ds(pl.multiple_of(other_y * pack, pack), pack)

    def y_copy(c, t):
        return pltpu.make_async_remote_copy(
            src_ref=y_out.at[c, t], dst_ref=y_in.at[c, t],
            send_sem=y_send.at[c, t], recv_sem=y_recv.at[c, t],
            device_id=(z * 2 + other_y, me_w), device_id_type=MESH,
        )

    def near_copy(j, t):
        return pltpu.make_async_remote_copy(
            src_ref=near_out.at[j, t], dst_ref=near_in.at[j, t],
            send_sem=near_send.at[j, t], recv_sem=near_recv.at[j, t],
            device_id=(near_z * 2 + y, me_w), device_id_type=MESH,
        )

    def kv_copy(j):
        return pltpu.make_async_remote_copy(
            src_ref=kv_out.at[j], dst_ref=kv_in.at[j],
            send_sem=kv_send.at[j], recv_sem=kv_recv.at[j],
            device_id=(near_z * 2 + y, me_w), device_id_type=MESH,
        )

    def mid_copy(t):
        return pltpu.make_async_remote_copy(
            src_ref=mid_out.at[t], dst_ref=mid_in.at[t],
            send_sem=mid_send.at[t], recv_sem=mid_recv.at[t],
            device_id=(mid_z * 2 + y, me_w), device_id_type=MESH,
        )

    def chunk(c):
        return pl.ds(pl.multiple_of(order[c] * 2 * pack, 2 * pack), 2 * pack)

    def product(c, t):
        return jnp.dot(rows[chunk(c), :], weights[t], preferred_element_type=jnp.float32)

    def multiply_kv(c):
        if c % 2:
            kv_out[c // 2] = product(c, q_tiles).astype(jnp.bfloat16)
            kv_copy(c // 2).start()
        else:
            own[c, q_tiles] = product(c, q_tiles)

    def make_tables():
        places_i = lax.broadcasted_iota(jnp.int32, (pack, pack), 0)
        places_j = lax.broadcasted_iota(jnp.int32, (pack, pack), 1)
        seg_j = jnp.broadcast_to(seg_ref[...], (pack, pack))
        same = seg_j.T == seg_j
        allowed[...] = jnp.where(same & (places_j <= places_i), 1.0, 0.0)
        start = jnp.min(jnp.where(same, places_j, pack).astype(jnp.float32), axis=1, keepdims=True)
        shape = (pack, HEAD_DIM)
        position = lax.broadcasted_iota(jnp.int32, shape, 0).astype(jnp.float32) - start
        lane = lax.broadcasted_iota(jnp.int32, shape, 1)
        half_dim = HEAD_DIM // 2
        ratio = (lane % half_dim).astype(jnp.float32) * (2.0 / HEAD_DIM)
        angles = position * jnp.exp(-math.log(ROPE_BASE) * ratio)
        cosine[...] = jnp.cos(angles)
        sine[...] = jnp.where(lane < half_dim, -1.0, 1.0) * jnp.sin(angles)

    def multiply(c, start, first_tile=0, last_tile=q_tiles):
        @pl.loop(first_tile, last_tile)
        def _(t):
            own[c, t] = product(c, t)
            y_out[c, t] = own[c, t, other_rows, :].astype(jnp.bfloat16)
            if start:
                y_copy(c, t).start()

    def pair_sum(c, t):
        y_copy(c, t).wait_recv()
        return own[c, t, own_rows, :] + y_in[c, t].astype(jnp.float32)

    def pass_near(j, y_next):
        for t in range(q_tiles):
            total = pair_sum(2 * j + 1, t)
            if t < len(y_next):
                y_copy(*y_next[t]).start()
            near_out[j, t] = total.astype(jnp.bfloat16)
            near_copy(j, t).start()

    def ready(*chunks):
        for step in (forward, relay, collect):
            for c in chunks:
                step(2 * c)
                step(2 * c + 1)

    ready(0)
    for load in loads:
        load.wait()
    multiply(0, True, 0, q_tiles - 1)
    ready(1)
    multiply(1, True)
    multiply_kv(1)
    ready(2, 3)
    multiply(2, True, 0, q_tiles // 2)
    multiply_kv(3)
    multiply(2, False, q_tiles // 2)
    pass_near(0, [(2, t) for t in range(q_tiles // 2, q_tiles)])
    multiply_kv(2)
    multiply_kv(0)
    multiply(3, False)
    multiply(0, False, q_tiles - 1)
    for c, j in ((2, 0), (0, 1)):
        kv_copy(j).wait_recv()
        own[c, q_tiles] = own[c, q_tiles] + kv_in[j].astype(jnp.float32)
        y_out[c, q_tiles] = own[c, q_tiles, other_rows, :].astype(jnp.bfloat16)

    make_tables()
    y_later = [(2, q_tiles), (0, q_tiles)] + [(3, t) for t in range(q_tiles)]
    for t in range(q_tiles):
        total = pair_sum(2, t)
        y_copy(*y_later[t]).start()
        near_copy(0, t).wait_recv()
        mid_out[t] = (total + near_in[0, t].astype(jnp.float32)).astype(jnp.bfloat16)
        mid_copy(t).start()

    mid_out[q_tiles] = pair_sum(2, q_tiles).astype(jnp.bfloat16)
    mid_copy(q_tiles).start()
    for later in y_later[q_tiles:]:
        y_copy(*later).start()
    pass_near(1, [(0, q_tiles - 1)])

    def rope(head):
        return head * cosine[...] + pltpu.roll(head, HEAD_DIM // 2, 1) * sine[...]

    kv_total = pair_sum(0, q_tiles)
    mid_copy(q_tiles).wait_recv()
    kv_total = (kv_total + mid_in[q_tiles].astype(jnp.float32)).astype(jnp.bfloat16)
    kv_heads = kv // HEAD_DIM
    for h in range(kv_heads):
        first_col = h * HEAD_DIM
        key_head = kv_total[:, first_col : first_col + HEAD_DIM].astype(jnp.float32)
        held_keys[h] = rope(key_head).astype(jnp.bfloat16)
        held_values[h] = kv_total[:, kv + first_col : kv + first_col + HEAD_DIM]

    @pl.loop(0, q_tiles)
    def _(t):
        total = pair_sum(0, t)
        mid_copy(t).wait_recv()
        total = total + mid_in[t].astype(jnp.float32)
        near_copy(1, t).wait_recv()
        total = total + near_in[1, t].astype(jnp.float32)
        kv_head = t * kv_heads // q_tiles
        keys, values = held_keys[kv_head], held_values[kv_head]
        mixed = []
        for h in range(TILE // HEAD_DIM):
            head = rope(total[:, h * HEAD_DIM : (h + 1) * HEAD_DIM]).astype(jnp.bfloat16)
            scores = lax.dot_general(
                head, keys, (((1,), (1,)), ((), ())), preferred_element_type=jnp.float32
            ) * HEAD_DIM ** (-0.5)
            chances = jnp.where(allowed[...] > 0.0, jnp.exp(scores), 0.0)
            chances = chances * (1.0 / jnp.sum(chances, axis=1, keepdims=True))
            mixed.append(
                jnp.dot(chances.astype(jnp.bfloat16), values, preferred_element_type=jnp.float32)
            )
        columns = pl.ds(pl.multiple_of(t * TILE, TILE), TILE)
        out_ref[:, columns] = jnp.concatenate(mixed, axis=1).astype(jnp.bfloat16)

    for copy in sent:
        copy.wait_send()

    @pl.loop(0, q_tiles)
    def _(t):
        for c in range(4):
            y_copy(c, t).wait_send()
        for j in range(2):
            near_copy(j, t).wait_send()
        mid_copy(t).wait_send()

    for j in range(2):
        kv_copy(j).wait_send()
        y_copy(2 * j, q_tiles).wait_send()
    mid_copy(q_tiles).wait_send()


def attend_on_slice(tokens, segment_ids, norm_gain, query_weight, key_weight, value_weight):
    count, features = tokens.shape
    slab, query_cols = query_weight.shape
    tiles = query_cols // TILE + 1
    pack = 4 * count
    bf16, f32 = jnp.bfloat16, jnp.float32
    dma = pltpu.SemaphoreType.DMA
    vmem = pl.BlockSpec(memory_space=pltpu.VMEM)
    hbm = pl.BlockSpec(memory_space=pltpu.HBM)
    return pl.pallas_call(
        attend_kernel,
        out_shape=jax.ShapeDtypeStruct((pack, query_cols), bf16),
        in_specs=[hbm] * 5 + [vmem],
        out_specs=vmem,
        scratch_shapes=[
            pltpu.VMEM((count, features), bf16),
            pltpu.VMEM((1, features), f32),
            pltpu.VMEM((tiles, slab, TILE), bf16),
            pltpu.VMEM((8, count, slab), bf16),
            pltpu.VMEM((8 * pack, slab), bf16),
            pltpu.VMEM((4, tiles, 2 * pack, TILE), f32),
            pltpu.VMEM((4, tiles, pack, TILE), bf16),
            pltpu.VMEM((4, tiles, pack, TILE), bf16),
            pltpu.VMEM((2, tiles - 1, pack, TILE), bf16),
            pltpu.VMEM((2, tiles - 1, pack, TILE), bf16),
            pltpu.VMEM((2, 2 * pack, TILE), bf16),
            pltpu.VMEM((2, 2 * pack, TILE), bf16),
            pltpu.VMEM((tiles, pack, TILE), bf16),
            pltpu.VMEM((tiles, pack, TILE), bf16),
            pltpu.VMEM((TILE // 2 // HEAD_DIM, pack, HEAD_DIM), bf16),
            pltpu.VMEM((TILE // 2 // HEAD_DIM, pack, HEAD_DIM), bf16),
            pltpu.VMEM((pack, HEAD_DIM), f32),
            pltpu.VMEM((pack, HEAD_DIM), f32),
            pltpu.VMEM((pack, pack), f32),
            dma((tiles + 3,)),
            dma((8,)),
            dma((32,)),
            dma((8,)),
            dma((8,)),
            dma((8,)),
            dma((4, tiles)),
            dma((4, tiles)),
            dma((2, tiles - 1)),
            dma((2, tiles - 1)),
            dma((2,)),
            dma((2,)),
            dma((tiles,)),
            dma((tiles,)),
        ],
        compiler_params=pltpu.CompilerParams(
            collective_id=0, has_side_effects=True, vmem_limit_bytes=53 * 1024 * 1024
        ),
        cost_estimate=pl.CostEstimate(
            flops=2 * 8 * pack * slab * tiles * TILE, bytes_accessed=2 * slab * tiles * TILE, transcendentals=0
        ),
    )(
        tokens, norm_gain[None, :], query_weight, key_weight, value_weight,
        segment_ids[None, :],
    )


def per_device(tokens, segment_ids, norm_gain, query_weight, key_weight, value_weight):
    head_dim = HEAD_DIM
    query_cols = query_weight.shape[1]
    heads_dev = query_cols // head_dim
    group_size = HEADS // KV_HEADS
    local_kv = max(1, heads_dev // group_size)
    first_kv = lax.axis_index("weight") * heads_dev // group_size
    key_width = local_kv * head_dim
    if (lax.axis_size("batch"), lax.axis_size("weight"), 2 * key_width) == (8, 4, TILE):
        return attend_on_slice(tokens, segment_ids, norm_gain, query_weight, key_weight, value_weight)
    key_block = lax.dynamic_slice_in_dim(key_weight, first_kv * head_dim, key_width, 1)
    value_block = lax.dynamic_slice_in_dim(value_weight, first_kv * head_dim, key_width, 1)
    values = tokens.astype(jnp.float32)
    inverse_rms = lax.rsqrt(jnp.mean(values * values, axis=1, keepdims=True) + EPSILON)
    normed = (values * inverse_rms * norm_gain[None, :]).astype(jnp.bfloat16)
    local_weights = jnp.concatenate([query_weight, key_block, value_block], axis=1)
    full_weights = lax.all_gather(local_weights, "batch", axis=0, tiled=True)
    projected = jnp.dot(
        lax.all_gather(normed, "weight", axis=0, tiled=True),
        full_weights,
        preferred_element_type=jnp.float32,
    )
    query_part = projected[:, :query_cols]
    key_rows = projected[:, query_cols : query_cols + key_width].astype(jnp.bfloat16)
    value_rows = projected[:, query_cols + key_width :].astype(jnp.bfloat16)
    pack_rows = segment_ids.shape[0]
    positions = positions_in_segment(segment_ids)
    queries = rotate(query_part.reshape(pack_rows, heads_dev, head_dim), positions).astype(
        jnp.bfloat16
    )
    rotated_keys = rotate(
        key_rows.astype(jnp.float32).reshape(pack_rows, local_kv, head_dim), positions
    ).astype(jnp.bfloat16)
    grouped = queries.reshape(pack_rows, local_kv, heads_dev // local_kv, head_dim)
    attended = attend(
        grouped, rotated_keys, value_rows.reshape(pack_rows, local_kv, head_dim), segment_ids
    )
    return attended.reshape(pack_rows, query_cols)


def solution(mesh):
    placed = (
        P(("batch", "weight"), None),
        P("batch"),
        P(),
        P("batch", "weight"),
        P("batch", None),
        P("batch", None),
    )
    return jax.shard_map(
        per_device, mesh=mesh, in_specs=placed, out_specs=P("batch", "weight"), check_vma=False
    )
```

```python
import math

import jax
import jax.numpy as jnp
from jax import lax
from jax.experimental import pallas as pl
from jax.experimental.pallas import tpu as pltpu
from jax.sharding import PartitionSpec as P

HEADS = 64
KV_HEADS = 8
HEAD_DIM = 128


ROPE_BASE = 500000.0
EPSILON = 1e-05


def positions_in_segment(seg_ids):
    places = jnp.arange(seg_ids.shape[0], dtype=jnp.int32)
    earlier = jnp.concatenate([seg_ids[:1] - 1, seg_ids[:-1]])
    starts = jnp.where(seg_ids != earlier, places, 0)
    leading = lax.cummax(starts, axis=0)
    return places - leading


def rope_tables(positions, head_dim):
    ratios = jnp.arange(head_dim // 2, dtype=jnp.float32) * (2.0 / head_dim)
    frequency = jnp.exp(-math.log(ROPE_BASE) * ratios)
    angles = positions.astype(jnp.float32)[:, None] * frequency[None, :]
    return jnp.cos(angles), jnp.sin(angles)


def rotate(vectors, positions):
    half_dim = vectors.shape[-1] // 2
    cosine, sine_part = rope_tables(positions, vectors.shape[-1])
    cosine, sine_part = cosine[:, None, :], sine_part[:, None, :]
    front_half = vectors[..., :half_dim]
    back_half = vectors[..., half_dim:]
    return jnp.concatenate(
        [front_half * cosine - back_half * sine_part, back_half * cosine + front_half * sine_part],
        axis=-1,
    )


def attend(grouped, rotated_keys, value_rows, seg_ids):
    scores = jnp.einsum(
        "ingd,jnd->ngij", grouped, rotated_keys, preferred_element_type=jnp.float32
    ) * grouped.shape[-1] ** (-0.5)
    places = jnp.arange(seg_ids.shape[0], dtype=jnp.int32)
    allowed = (seg_ids[:, None] == seg_ids[None, :]) & (places[None, :] <= places[:, None])
    weights = jnp.where(allowed, jnp.exp(scores), 0.0)
    probabilities = (weights / jnp.sum(weights, axis=-1, keepdims=True)).astype(jnp.bfloat16)
    mixed = jnp.einsum(
        "ngij,jnd->ingd", probabilities, value_rows, preferred_element_type=jnp.float32
    )
    return mixed.astype(jnp.bfloat16)


MESH = pl.DeviceIdType.MESH
TILE = 512


def attend_kernel(
    tokens_ref, gain_ref, query_ref, key_ref, value_ref, seg_ref, out_ref,
    tokens, gain, weights, normed, rows, own, y_out, y_in, near_out, near_in, kv_out, kv_in, mid_out, mid_in, held_keys, held_values, cosine, sine, allowed,
    load_sem, tok_send, tok_recv, x_send, core_send, relay_send,
    y_send, y_recv, near_send, near_recv, kv_send, kv_recv, mid_send, mid_recv,
):
    me_b = lax.axis_index("batch")
    me_w = lax.axis_index("weight")
    z, y = me_b // 2, me_b % 2
    count, features = tokens_ref.shape
    slab = query_ref.shape[0]
    pack = 4 * count
    tiles = weights.shape[0]
    q_tiles = tiles - 1
    kv = TILE // 2

    near_z, mid_z = z + 1 - 2 * (z % 2), (z + 2) % 4
    order = [z, 3 - z, mid_z, near_z]
    other_y = 1 - y
    sources = [(zz * 2 + y, zz * 2 + other_y) for zz in order]
    peers = [b for pair in sources for b in pair]
    x_w, core_w, far_w = (me_w + 2) % 4, me_w + 1 - 2 * (me_w % 2), 3 - me_w

    barrier = pltpu.get_barrier_semaphore()
    for i, b in enumerate(peers):
        if i != 0:
            pl.semaphore_signal(barrier, inc=1, device_id=(b, me_w), device_id_type=MESH)
    for w in (x_w, core_w):
        pl.semaphore_signal(barrier, inc=1, device_id=(me_b, w), device_id_type=MESH)

    token_load = pltpu.make_async_copy(tokens_ref, tokens, load_sem.at[tiles + 1])
    gain_load = pltpu.make_async_copy(gain_ref, gain, load_sem.at[tiles + 2])
    token_load.start()
    gain_load.start()
    loads = [
        pltpu.make_async_copy(
            query_ref.at[:, pl.ds(t * TILE, TILE)], weights.at[t], load_sem.at[t]
        )
        for t in range(q_tiles)
    ]
    first = pl.ds(pl.multiple_of(me_w * kv, kv), kv)
    loads.append(
        pltpu.make_async_copy(
            key_ref.at[:, first], weights.at[q_tiles, :, pl.ds(0, kv)], load_sem.at[q_tiles]
        )
    )
    loads.append(
        pltpu.make_async_copy(
            value_ref.at[:, first], weights.at[q_tiles, :, pl.ds(kv, kv)], load_sem.at[tiles]
        )
    )
    for load in loads:
        load.start()

    token_load.wait()
    gain_load.wait()
    total = jnp.zeros((count, 1), jnp.float32)
    for k in range(features // slab):
        part = tokens[:, k * slab : (k + 1) * slab].astype(jnp.float32)
        total = total + jnp.sum(part * part, axis=1, keepdims=True)
    inverse_rms = lax.rsqrt(total * (1.0 / features) + EPSILON)
    for k in range(features // slab):
        part = tokens[:, k * slab : (k + 1) * slab].astype(jnp.float32)
        normed[k] = (part * inverse_rms * gain[:, k * slab : (k + 1) * slab]).astype(jnp.bfloat16)

    def slot(b, w):
        return b * 4 + w

    def at_slot(s):
        return rows.at[pl.ds(pl.multiple_of(s * count, count), count)]

    def send(src, s, device, send_sem):
        return pltpu.make_async_remote_copy(
            src_ref=src, dst_ref=at_slot(s), send_sem=send_sem, recv_sem=tok_recv.at[s],
            device_id=device, device_id_type=MESH,
        )

    def arrived(s):
        send(at_slot(s), s, (me_b, x_w), x_send.at[0]).wait_recv()

    pl.semaphore_wait(barrier, 9)
    mine = slot(me_b, me_w)
    sent = []
    for i, b in enumerate(peers):
        if i != 0:
            copy = send(normed.at[b], mine, (b, me_w), tok_send.at[i])
            copy.start()
            sent.append(copy)
    rows[pl.ds(pl.multiple_of(mine * count, count), count), :] = normed[me_b]

    def forward(i):
        b = peers[i]
        s = slot(b, me_w)
        if i != 0:
            arrived(s)
        for w, sem in ((x_w, x_send), (core_w, core_send)):
            copy = send(at_slot(s), s, (me_b, w), sem.at[i])
            copy.start()
            sent.append(copy)

    def relay(i):
        s = slot(peers[i], x_w)
        arrived(s)
        copy = send(at_slot(s), s, (me_b, core_w), relay_send.at[i])
        copy.start()
        sent.append(copy)

    def collect(i):
        arrived(slot(peers[i], core_w))
        arrived(slot(peers[i], far_w))

    own_rows = pl.ds(pl.multiple_of(y * pack, pack), pack)
    other_rows = pl.ds(pl.multiple_of(other_y * pack, pack), pack)

    def y_copy(c, t):
        return pltpu.make_async_remote_copy(
            src_ref=y_out.at[c, t], dst_ref=y_in.at[c, t],
            send_sem=y_send.at[c, t], recv_sem=y_recv.at[c, t],
            device_id=(z * 2 + other_y, me_w), device_id_type=MESH,
        )

    def near_copy(j, t):
        return pltpu.make_async_remote_copy(
            src_ref=near_out.at[j, t], dst_ref=near_in.at[j, t],
            send_sem=near_send.at[j, t], recv_sem=near_recv.at[j, t],
            device_id=(near_z * 2 + y, me_w), device_id_type=MESH,
        )

    def kv_copy(j):
        return pltpu.make_async_remote_copy(
            src_ref=kv_out.at[j], dst_ref=kv_in.at[j],
            send_sem=kv_send.at[j], recv_sem=kv_recv.at[j],
            device_id=(near_z * 2 + y, me_w), device_id_type=MESH,
        )

    def mid_copy(t):
        return pltpu.make_async_remote_copy(
            src_ref=mid_out.at[t], dst_ref=mid_in.at[t],
            send_sem=mid_send.at[t], recv_sem=mid_recv.at[t],
            device_id=(mid_z * 2 + y, me_w), device_id_type=MESH,
        )

    def chunk(c):
        return pl.ds(pl.multiple_of(order[c] * 2 * pack, 2 * pack), 2 * pack)

    def product(c, t):
        return jnp.dot(rows[chunk(c), :], weights[t], preferred_element_type=jnp.float32)

    def multiply_kv(c):
        if c % 2:
            kv_out[c // 2] = product(c, q_tiles).astype(jnp.bfloat16)
            kv_copy(c // 2).start()
        else:
            own[c, q_tiles] = product(c, q_tiles)

    def make_tables():
        places_i = lax.broadcasted_iota(jnp.int32, (pack, pack), 0)
        places_j = lax.broadcasted_iota(jnp.int32, (pack, pack), 1)
        seg_j = jnp.broadcast_to(seg_ref[...], (pack, pack))
        same = seg_j.T == seg_j
        allowed[...] = jnp.where(same & (places_j <= places_i), 1.0, 0.0)
        start = jnp.min(jnp.where(same, places_j, pack).astype(jnp.float32), axis=1, keepdims=True)
        shape = (pack, HEAD_DIM)
        position = lax.broadcasted_iota(jnp.int32, shape, 0).astype(jnp.float32) - start
        lane = lax.broadcasted_iota(jnp.int32, shape, 1)
        half_dim = HEAD_DIM // 2
        ratio = (lane % half_dim).astype(jnp.float32) * (2.0 / HEAD_DIM)
        angles = position * jnp.exp(-math.log(ROPE_BASE) * ratio)
        cosine[...] = jnp.cos(angles)
        sine[...] = jnp.where(lane < half_dim, -1.0, 1.0) * jnp.sin(angles)

    def multiply(c, start, first_tile=0, last_tile=q_tiles):
        @pl.loop(first_tile, last_tile)
        def _(t):
            own[c, t] = product(c, t)
            y_out[c, t] = own[c, t, other_rows, :].astype(jnp.bfloat16)
            if start:
                y_copy(c, t).start()

    def pair_sum(c, t):
        y_copy(c, t).wait_recv()
        return own[c, t, own_rows, :] + y_in[c, t].astype(jnp.float32)

    def pass_near(j, y_next):
        for t in range(q_tiles):
            total = pair_sum(2 * j + 1, t)
            if t < len(y_next):
                y_copy(*y_next[t]).start()
            near_out[j, t] = total.astype(jnp.bfloat16)
            near_copy(j, t).start()

    def run(step, *chunks):
        for c in chunks:
            step(2 * c)
            step(2 * c + 1)

    run(forward, 0, 1)
    run(relay, 0)
    run(collect, 0)
    for load in loads:
        load.wait()
    multiply(0, True, 0, q_tiles // 2)
    run(relay, 1)
    run(collect, 1)
    multiply(1, True)
    run(forward, 2, 3)
    multiply_kv(1)
    run(relay, 2, 3)
    run(collect, 2, 3)
    multiply_kv(3)
    multiply(2, False)
    pass_near(0, [(2, t) for t in range(q_tiles)])
    multiply_kv(2)
    multiply_kv(0)
    multiply(3, False)
    multiply(0, False, q_tiles // 2)
    for c, j in ((2, 0), (0, 1)):
        kv_copy(j).wait_recv()
        own[c, q_tiles] = own[c, q_tiles] + kv_in[j].astype(jnp.float32)
        y_out[c, q_tiles] = own[c, q_tiles, other_rows, :].astype(jnp.bfloat16)

    make_tables()
    y_later = [(2, q_tiles), (0, q_tiles)] + [(3, t) for t in range(q_tiles)]
    for t in range(q_tiles):
        total = pair_sum(2, t)
        y_copy(*y_later[t]).start()
        near_copy(0, t).wait_recv()
        mid_out[t] = (total + near_in[0, t].astype(jnp.float32)).astype(jnp.bfloat16)
        mid_copy(t).start()

    mid_out[q_tiles] = pair_sum(2, q_tiles).astype(jnp.bfloat16)
    mid_copy(q_tiles).start()
    for later in y_later[q_tiles:]:
        y_copy(*later).start()
    pass_near(1, [(0, t) for t in range(q_tiles // 2, q_tiles)])

    def rope(head):
        return head * cosine[...] + pltpu.roll(head, HEAD_DIM // 2, 1) * sine[...]

    kv_total = pair_sum(0, q_tiles)
    mid_copy(q_tiles).wait_recv()
    kv_total = (kv_total + mid_in[q_tiles].astype(jnp.float32)).astype(jnp.bfloat16)
    kv_heads = kv // HEAD_DIM
    for h in range(kv_heads):
        first_col = h * HEAD_DIM
        key_head = kv_total[:, first_col : first_col + HEAD_DIM].astype(jnp.float32)
        held_keys[h] = rope(key_head).astype(jnp.bfloat16)
        held_values[h] = kv_total[:, kv + first_col : kv + first_col + HEAD_DIM]

    @pl.loop(0, q_tiles)
    def _(t):
        total = pair_sum(0, t)
        mid_copy(t).wait_recv()
        total = total + mid_in[t].astype(jnp.float32)
        near_copy(1, t).wait_recv()
        total = total + near_in[1, t].astype(jnp.float32)
        kv_head = t * kv_heads // q_tiles
        keys, values = held_keys[kv_head], held_values[kv_head]
        mixed = []
        for h in range(TILE // HEAD_DIM):
            head = rope(total[:, h * HEAD_DIM : (h + 1) * HEAD_DIM]).astype(jnp.bfloat16)
            scores = lax.dot_general(
                head, keys, (((1,), (1,)), ((), ())), preferred_element_type=jnp.float32
            ) * HEAD_DIM ** (-0.5)
            chances = jnp.where(allowed[...] > 0.0, jnp.exp(scores), 0.0)
            chances = chances * (1.0 / jnp.sum(chances, axis=1, keepdims=True))
            mixed.append(
                jnp.dot(chances.astype(jnp.bfloat16), values, preferred_element_type=jnp.float32)
            )
        columns = pl.ds(pl.multiple_of(t * TILE, TILE), TILE)
        out_ref[:, columns] = jnp.concatenate(mixed, axis=1).astype(jnp.bfloat16)

    for copy in sent:
        copy.wait_send()

    @pl.loop(0, q_tiles)
    def _(t):
        for c in range(4):
            y_copy(c, t).wait_send()
        for j in range(2):
            near_copy(j, t).wait_send()
        mid_copy(t).wait_send()

    for j in range(2):
        kv_copy(j).wait_send()
        y_copy(2 * j, q_tiles).wait_send()
    mid_copy(q_tiles).wait_send()


def attend_on_slice(tokens, segment_ids, norm_gain, query_weight, key_weight, value_weight):
    count, features = tokens.shape
    slab, query_cols = query_weight.shape
    tiles = query_cols // TILE + 1
    pack = 4 * count
    bf16, f32 = jnp.bfloat16, jnp.float32
    dma = pltpu.SemaphoreType.DMA
    vmem = pl.BlockSpec(memory_space=pltpu.VMEM)
    hbm = pl.BlockSpec(memory_space=pltpu.HBM)
    return pl.pallas_call(
        attend_kernel,
        out_shape=jax.ShapeDtypeStruct((pack, query_cols), bf16),
        in_specs=[hbm] * 5 + [vmem],
        out_specs=vmem,
        scratch_shapes=[
            pltpu.VMEM((count, features), bf16),
            pltpu.VMEM((1, features), f32),
            pltpu.VMEM((tiles, slab, TILE), bf16),
            pltpu.VMEM((8, count, slab), bf16),
            pltpu.VMEM((8 * pack, slab), bf16),
            pltpu.VMEM((4, tiles, 2 * pack, TILE), f32),
            pltpu.VMEM((4, tiles, pack, TILE), bf16),
            pltpu.VMEM((4, tiles, pack, TILE), bf16),
            pltpu.VMEM((2, tiles - 1, pack, TILE), bf16),
            pltpu.VMEM((2, tiles - 1, pack, TILE), bf16),
            pltpu.VMEM((2, 2 * pack, TILE), bf16),
            pltpu.VMEM((2, 2 * pack, TILE), bf16),
            pltpu.VMEM((tiles, pack, TILE), bf16),
            pltpu.VMEM((tiles, pack, TILE), bf16),
            pltpu.VMEM((TILE // 2 // HEAD_DIM, pack, HEAD_DIM), bf16),
            pltpu.VMEM((TILE // 2 // HEAD_DIM, pack, HEAD_DIM), bf16),
            pltpu.VMEM((pack, HEAD_DIM), f32),
            pltpu.VMEM((pack, HEAD_DIM), f32),
            pltpu.VMEM((pack, pack), f32),
            dma((tiles + 3,)),
            dma((8,)),
            dma((32,)),
            dma((8,)),
            dma((8,)),
            dma((8,)),
            dma((4, tiles)),
            dma((4, tiles)),
            dma((2, tiles - 1)),
            dma((2, tiles - 1)),
            dma((2,)),
            dma((2,)),
            dma((tiles,)),
            dma((tiles,)),
        ],
        compiler_params=pltpu.CompilerParams(
            collective_id=0, has_side_effects=True, vmem_limit_bytes=53 * 1024 * 1024
        ),
        cost_estimate=pl.CostEstimate(
            flops=2 * 8 * pack * slab * tiles * TILE, bytes_accessed=2 * slab * tiles * TILE, transcendentals=0
        ),
    )(
        tokens, norm_gain[None, :], query_weight, key_weight, value_weight,
        segment_ids[None, :],
    )


def per_device(tokens, segment_ids, norm_gain, query_weight, key_weight, value_weight):
    head_dim = HEAD_DIM
    query_cols = query_weight.shape[1]
    heads_dev = query_cols // head_dim
    group_size = HEADS // KV_HEADS
    local_kv = max(1, heads_dev // group_size)
    first_kv = lax.axis_index("weight") * heads_dev // group_size
    key_width = local_kv * head_dim
    if (lax.axis_size("batch"), lax.axis_size("weight"), 2 * key_width) == (8, 4, TILE):
        return attend_on_slice(tokens, segment_ids, norm_gain, query_weight, key_weight, value_weight)
    key_block = lax.dynamic_slice_in_dim(key_weight, first_kv * head_dim, key_width, 1)
    value_block = lax.dynamic_slice_in_dim(value_weight, first_kv * head_dim, key_width, 1)
    values = tokens.astype(jnp.float32)
    inverse_rms = lax.rsqrt(jnp.mean(values * values, axis=1, keepdims=True) + EPSILON)
    normed = (values * inverse_rms * norm_gain[None, :]).astype(jnp.bfloat16)
    local_weights = jnp.concatenate([query_weight, key_block, value_block], axis=1)
    full_weights = lax.all_gather(local_weights, "batch", axis=0, tiled=True)
    projected = jnp.dot(
        lax.all_gather(normed, "weight", axis=0, tiled=True),
        full_weights,
        preferred_element_type=jnp.float32,
    )
    query_part = projected[:, :query_cols]
    key_rows = projected[:, query_cols : query_cols + key_width].astype(jnp.bfloat16)
    value_rows = projected[:, query_cols + key_width :].astype(jnp.bfloat16)
    pack_rows = segment_ids.shape[0]
    positions = positions_in_segment(segment_ids)
    queries = rotate(query_part.reshape(pack_rows, heads_dev, head_dim), positions).astype(
        jnp.bfloat16
    )
    rotated_keys = rotate(
        key_rows.astype(jnp.float32).reshape(pack_rows, local_kv, head_dim), positions
    ).astype(jnp.bfloat16)
    grouped = queries.reshape(pack_rows, local_kv, heads_dev // local_kv, head_dim)
    attended = attend(
        grouped, rotated_keys, value_rows.reshape(pack_rows, local_kv, head_dim), segment_ids
    )
    return attended.reshape(pack_rows, query_cols)


def solution(mesh):
    placed = (
        P(("batch", "weight"), None),
        P("batch"),
        P(),
        P("batch", "weight"),
        P("batch", None),
        P("batch", None),
    )
    return jax.shard_map(
        per_device, mesh=mesh, in_specs=placed, out_specs=P("batch", "weight"), check_vma=False
    )
```
